256 devices in a mesh: seg: 8 (over z), tile: 32 (over x, y, core).
Axes of the slice: x: 4, y: 4, z: 8, core: 2. Of those that a mesh axis runs over, the one named last changes fastest.
Arguments:
- floc_attr: float32 [8, 4194304], P(None, ('seg', 'tile')), may hold values from -4 to 4, as said below
- floc_slot: int32 [4194304], P(('seg', 'tile')), may hold values from 0 to 32767, as said below
- same_pairs: int32 [8, 32, 2, 1024], P('seg', 'tile'), may hold values from 0 to 255, as said below
- same_count: int32 [8, 32], P('seg', 'tile'), may hold values from 128 to 1024, as said below
- adj_pairs: int32 [8, 32, 2, 128], P('seg', 'tile'), may hold values from 0 to 255, as said below
- neighbour_pair_count: int32 [8, 32], P('seg', 'tile'), may hold values from 32 to 128, as said below
Outputs:
- new_mass: float32 [4194304], P(('seg', 'tile'))
The draws below stay inside these ranges and needn't reach their ends.
Inputs may be any that keep to these rules, and one draw needn't show every extreme that they name: `floc_slot`: on each owner the 16384 slots are distinct; in every segment one tile is sent 1024 flocs by every tile of the segment, which makes its buffer full. `same_pairs`: pairs of blocks of one cell owner; the partner lies within two blocks of the receiving block. `same_count`: some owner uses all 1024 entries. `adj_pairs`: A partner below 32 comes with an own block below 32; a partner of 32 or more with an own block of 224 or more. `neighbour_pair_count`: some owner uses all 128 entries. `floc_attr`: rows 0 to 5 are coordinates, row 6 masses, row 7 radii; masses and radii are positive.
All inputs are finite; a program needn't handle non-finite values.
Results may differ from the reference program's by a relative error of at most 0.0003.
Values sent between devices are 32-bit elements; how exact they have to be, the bound alone decides.
No kernel may reach another device: no remote copies, remote signals or barrier semaphores. Data moves between devices by JAX's collectives and lax.ppermute only.
A program may use at most 128 MiB of HBM per device.

```python
import jax
import jax.numpy as jnp
from jax import lax

ATTR = 8
BLOCK = 128
FLOC_DEV = 16384
SEGS = 8
TILES = 32
DEVS = 256
TOTAL = 4194304
NBLK = 256
EDGE = 32
PSAME = 1024
PADJ = 128


def draw_floc_attr(key, part):
    cell_positions = jnp.clip(jax.random.normal(jax.random.fold_in(key, 1), (6, TOTAL), jnp.float32), -4.0, 4.0)
    mass = 0.2 * 10.0 ** jax.random.uniform(jax.random.fold_in(key, 2), (1, TOTAL), jnp.float32, 0.1, 0.9)
    radius = 0.5 * 4.0 ** jax.random.uniform(jax.random.fold_in(key, 3), (1, TOTAL), jnp.float32, 0.1, 0.9)
    return jnp.concatenate([cell_positions, mass, radius], 0)


def draw_floc_slot(key, part):
    cap = 2 * FLOC_DEV // TILES
    full = jax.random.randint(jax.random.fold_in(key, 11), (SEGS,), 0, TILES)

    def one(owner_id):
        inner = jax.random.fold_in(key, owner_id + 1000)
        target = full[owner_id // TILES]
        index = jnp.arange((TILES - 1) * cap, dtype=jnp.int32)
        other = index // cap
        dest = other + (other >= target).astype(jnp.int32)
        candidate = dest * cap + index % cap
        selected_pairs = jax.random.permutation(jax.random.fold_in(inner, 1), candidate)[:FLOC_DEV - cap]
        chosen = jnp.concatenate([target * cap + jnp.arange(cap, dtype=jnp.int32), selected_pairs])
        return jax.random.permutation(jax.random.fold_in(inner, 2), chosen)
    return jax.vmap(one)(jnp.arange(DEVS, dtype=jnp.int32)).reshape(TOTAL)


def draw_same_pairs(key, part):
    first = jax.random.randint(jax.random.fold_in(key, 21), (SEGS, TILES, 1, PSAME), 0, NBLK)
    offset = jax.random.randint(jax.random.fold_in(key, 22), (SEGS, TILES, 1, PSAME), -2, 3)
    second = jnp.clip(first + offset, 0, NBLK - 1)
    return jnp.concatenate([first, second], 2).astype(jnp.int32)


def draw_same_count(key, part):
    counts = jax.random.randint(jax.random.fold_in(key, 31), (DEVS,), PSAME // 8, PSAME + 1)
    where = jax.random.randint(jax.random.fold_in(key, 32), (), 0, DEVS)
    counts = jnp.where(jnp.arange(DEVS) == where, PSAME, counts)
    return counts.reshape(SEGS, TILES).astype(jnp.int32)


def draw_adj_pairs(key, part):
    partner = jax.random.randint(jax.random.fold_in(key, 41), (SEGS, TILES, 1, PADJ), 0, 2 * EDGE)
    local = jax.random.randint(jax.random.fold_in(key, 42), (SEGS, TILES, 1, PADJ), 0, EDGE)
    own = jnp.where(partner < EDGE, local, NBLK - EDGE + local)
    return jnp.concatenate([own, partner], 2).astype(jnp.int32)


def draw_neighbour_pair_count(key, part):
    counts = jax.random.randint(jax.random.fold_in(key, 51), (DEVS,), PADJ // 4, PADJ + 1)
    where = jax.random.randint(jax.random.fold_in(key, 52), (), 0, DEVS)
    counts = jnp.where(jnp.arange(DEVS) == where, PADJ, counts)
    return counts.reshape(SEGS, TILES).astype(jnp.int32)


def setup_inputs(seed: int = 0) -> dict:
    key_list = jax.random.split(jax.random.key(seed), 7)
    floc_attr = draw_floc_attr(jax.random.fold_in(key_list[6], 71), 0)
    floc_slot = draw_floc_slot(jax.random.fold_in(key_list[6], 71), 0)
    same_pairs = draw_same_pairs(jax.random.fold_in(key_list[6], 71), 0)
    same_count = draw_same_count(jax.random.fold_in(key_list[6], 71), 0)
    adj_pairs = draw_adj_pairs(jax.random.fold_in(key_list[6], 71), 0)
    neighbour_pair_count = draw_neighbour_pair_count(jax.random.fold_in(key_list[6], 71), 0)
    return dict(floc_attr=floc_attr, floc_slot=floc_slot, same_pairs=same_pairs, same_count=same_count, adj_pairs=adj_pairs, neighbour_pair_count=neighbour_pair_count)


WIDTH = 2.0
RATE = 0.05


def pairwise_gain_values(left, right, same_block):
    left_position = left[:, :6]
    right_position = right[:, :6]
    crossing_product = jnp.einsum("rmh,rmw->rhw", left_position, right_position, precision=lax.Precision.HIGHEST)
    norm_l = jnp.sum(left_position * left_position, axis=1)
    norm_r = jnp.sum(right_position * right_position, axis=1)
    dist = norm_l[:, :, None] + norm_r[:, None, :] - 2.0 * crossing_product
    reach = left[:, 7][:, :, None] + right[:, 7][:, None, :]
    weight = reach * reach * jnp.exp(-dist / WIDTH)
    diag = jnp.arange(BLOCK)[:, None] == jnp.arange(BLOCK)[None, :]
    weight = jnp.where(same_block[:, None, None] & diag[None], 0.0, weight)
    return jnp.einsum("gpq,gq->gp", weight, right[:, 6], precision=lax.Precision.HIGHEST)


def reference(floc_attr, floc_slot, same_pairs, same_count, adj_pairs, neighbour_pair_count):
    cap = 2 * FLOC_DEV // TILES
    cblk = cap // BLOCK
    attrs = floc_attr.reshape(ATTR, DEVS, FLOC_DEV).transpose(1, 2, 0)
    slots = floc_slot.reshape(DEVS, FLOC_DEV)

    def scatter_one(values, where):
        empty = jnp.zeros((NBLK, ATTR, BLOCK), jnp.float32)
        return empty.at[where // BLOCK, :, where % BLOCK].set(values)

    send = jax.vmap(scatter_one)(attrs, slots)
    send = send.reshape(SEGS, TILES, TILES, cblk, ATTR, BLOCK)
    owner = send.transpose(0, 2, 1, 3, 4, 5).reshape(SEGS, TILES, NBLK, ATTR, BLOCK)
    zero = jnp.zeros((1, TILES, EDGE, ATTR, BLOCK), jnp.float32)
    upper = jnp.concatenate([zero, owner[:-1, :, NBLK - EDGE:]], 0)
    lower = jnp.concatenate([owner[1:, :, :EDGE], zero], 0)
    table = jnp.concatenate([upper, owner, lower], 2).reshape(DEVS, NBLK + 2 * EDGE, ATTR, BLOCK)
    same = same_pairs.reshape(DEVS, 2, PSAME)
    adj = adj_pairs.reshape(DEVS, 2, PADJ)
    first = jnp.concatenate([same[:, 0] + EDGE, adj[:, 0] + EDGE], 1).astype(jnp.int32)
    partner = jnp.where(adj[:, 1] < EDGE, adj[:, 1], adj[:, 1] + NBLK)
    second = jnp.concatenate([same[:, 1] + EDGE, partner], 1).astype(jnp.int32)
    live_same = jnp.arange(PSAME)[None, :] < same_count.reshape(DEVS, 1)
    live_adj = jnp.arange(PADJ)[None, :] < neighbour_pair_count.reshape(DEVS, 1)
    live = jnp.concatenate([live_same, live_adj], 1)

    def one(items):
        tab, fi, se, li = items
        part = pairwise_gain_values(tab[fi], tab[se], fi == se)
        part = jnp.where(li[:, None], part, 0.0)
        acc = jnp.zeros((NBLK + 2 * EDGE, BLOCK), jnp.float32).at[fi].add(part)
        return acc[EDGE:EDGE + NBLK]

    gains = lax.map(one, (table, first, second, live))
    gains = gains.reshape(SEGS, TILES, TILES, cblk, BLOCK).transpose(0, 2, 1, 3, 4)
    gains = gains.reshape(DEVS, NBLK * BLOCK)
    selected_pairs = jnp.take_along_axis(gains, slots, axis=1)
    mass = floc_attr[6].reshape(DEVS, FLOC_DEV)
    return (mass + RATE * selected_pairs).reshape(TOTAL)
```

```python
import functools

import jax
import jax.numpy as jnp
import numpy as np
from jax import lax
from jax.experimental import pallas as pl
from jax.experimental.pallas import tpu as pltpu
from jax.sharding import PartitionSpec as P

ATTR = 8
BLOCK = 128
FLOC_DEV = 16384
NBLK = 256
EDGE = 32
RATE = 0.05
PSAME = 1024
PADJ = 128
SCALE = float(np.sqrt(np.log2(np.e)))
CHUNK = 1024
GCHUNK = 1024
KF = 48
SAME_UNROLL = 8
ADJ_UNROLL = 8
QROWS = 32
MIB = 2**20
BF = jnp.bfloat16
F32 = jnp.float32


def rounded(x):
    return x.astype(BF).astype(F32)


def onehot_rows(rows, index):
    shape = (rows, index.shape[1])
    return jnp.where(lax.broadcasted_iota(jnp.int32, shape, 0) == index, 1.0, 0.0)


def scatter_kernel(attr_ref, slot_ref, pairs_ref, count_ref, out_ref, mult_ref, y_ref, b_ref, acc_ref):
    first = pairs_ref[0:1, :]
    offset = pairs_ref[1:2, :] - first + 2
    live = lax.broadcasted_iota(jnp.int32, (1, PSAME), 1) < count_ref[0, 0]
    offset = jnp.where(live, offset, -1)
    mult_ref[...] = lax.dot_general(
        onehot_rows(8, offset).astype(BF),
        onehot_rows(NBLK, first).astype(BF),
        (((1,), (1,)), ((), ())),
        preferred_element_type=F32,
    )
    row = lax.broadcasted_iota(jnp.int32, (ATTR, CHUNK), 0)

    def step(s, carry):
        low = pl.multiple_of(s * CHUNK, CHUNK)
        slot = slot_ref[:, pl.ds(low, CHUNK)]
        block = onehot_rows(NBLK, slot >> 7).astype(BF)
        b_ref[:, :CHUNK] = block
        b_ref[:, CHUNK:] = block
        lane = lax.broadcasted_iota(jnp.int32, (BLOCK, CHUNK), 0) == (slot & 127)
        value = attr_ref[:, pl.ds(low, CHUNK)]
        value = jnp.where(row < 6, value * SCALE, value)
        high = rounded(value)
        rest = value - high
        for a in range(ATTR):
            at = slice(a * BLOCK, (a + 1) * BLOCK)
            y_ref[at, :CHUNK] = jnp.where(lane, high[a : a + 1], 0.0).astype(BF)
            y_ref[at, CHUNK:] = jnp.where(lane, rest[a : a + 1], 0.0).astype(BF)
        acc_ref[...] += lax.dot_general(
            y_ref[...], b_ref[...], (((1,), (1,)), ((), ())), preferred_element_type=F32
        )
        return carry

    acc_ref[...] = jnp.zeros_like(acc_ref)
    lax.fori_loop(0, FLOC_DEV // CHUNK, step, 0)
    for a in range(ATTR):
        out_ref[:, a, :] = acc_ref[a * BLOCK : (a + 1) * BLOCK, :].T


def forms(v):
    row = lax.broadcasted_iota(jnp.int32, (8, BLOCK), 0)
    six = row < 6
    lo3 = row < 3
    high = rounded(v)
    rest = v - high
    norm = -0.5 * jnp.sum(jnp.where(six, v * v, 0.0), axis=0, keepdims=True)
    radius = v[7:8]
    x = jnp.where(lo3, jnp.broadcast_to(norm, (8, BLOCK)), jnp.broadcast_to(radius * radius, (8, BLOCK)))
    p0 = rounded(x)
    p1 = rounded(x - p0)
    p2 = x - p0 - p1
    k = jnp.where(lo3, row, row - 3)
    own = jnp.where(six, jnp.where(k == 0, p0, jnp.where(k == 1, p1, p2)), 0.0)
    one = jnp.ones((8, BLOCK), F32)
    zero = jnp.zeros((8, BLOCK), F32)
    mid3 = (row >= 3) & six
    left = jnp.concatenate([high, high, rest, rest, own, jnp.where(six, one, zero)], axis=0)
    h6 = jnp.where(six, high, 0.0)
    m6 = jnp.where(six, rest, 0.0)
    h7 = jnp.where(row == 7, 2.0 * high, 0.0)
    m7 = jnp.where(row == 7, 2.0 * rest, 0.0)
    arg = [h6, m6, h6, m6, jnp.where(lo3, one, zero), jnp.where(lo3, own, 0.0)]
    reach = [h7, m7, h7, m7, jnp.where(mid3, one, zero), jnp.where(mid3, own, 0.0)]
    right = jnp.concatenate([jnp.concatenate(arg, axis=0), jnp.concatenate(reach, axis=0)], axis=1)
    return left, right


def partner_form(v, left, j, xt_ref, mb_ref):
    turned = jnp.concatenate([left, v], axis=0).T
    xt_ref[j] = turned[:, :KF].astype(BF)
    mb_ref[j] = jnp.broadcast_to(turned[:, KF + 6 : KF + 7], (BLOCK, BLOCK))


def same_kernel(o_ref, mult_ref, out_ref, xt_ref, r_ref, mb_ref):
    zero_right = jnp.zeros((KF, 2 * BLOCK), BF)
    r_ref[0] = zero_right
    r_ref[1] = zero_right

    def build(j, carry):
        v = o_ref[j]
        left, right = forms(v)
        r_ref[j + 2] = right.astype(BF)
        partner_form(v, left, j, xt_ref, mb_ref)
        return carry

    lax.fori_loop(0, NBLK, build, 0, unroll=4)
    lane = lax.broadcasted_iota(jnp.int32, (QROWS, BLOCK), 1)
    sub = lax.broadcasted_iota(jnp.int32, (QROWS, BLOCK), 0)

    def main(j, carry):
        f1, f2 = carry
        j1 = jnp.maximum(j - 1, 0)
        j2 = jnp.maximum(j - 2, 0)
        rhs = jnp.concatenate([r_ref[j + 2], r_ref[j + 1], r_ref[j]], axis=1)
        mass1 = o_ref[j1][6:7] * mult_ref[1, j]
        mass2 = o_ref[j2][6:7] * mult_ref[0, j]
        acc = [jnp.zeros((8, BLOCK), F32) for _ in range(3)]
        rev = []
        for q in range(BLOCK // QROWS):
            at = slice(q * QROWS, (q + 1) * QROWS)
            d = jnp.dot(xt_ref[j, at, :], rhs, preferred_element_type=F32)
            mb = mb_ref[j, at, :]
            w = []
            for a in range(3):
                low = a * 2 * BLOCK
                e = jnp.exp2(d[:, low : low + BLOCK]) * d[:, low + BLOCK : low + 2 * BLOCK]
                if a == 0:
                    e = jnp.where(lane == sub + q * QROWS, 0.0, e)
                w.append(e)
                acc[a] = acc[a] + jnp.sum((e * mb).reshape(QROWS // 8, 8, BLOCK), axis=0)
            rev.append(w[1] * mass1 + w[2] * mass2)
        back = jnp.sum(jnp.concatenate(rev, axis=0).T.reshape(BLOCK // 8, 8, BLOCK), axis=0)
        f0 = acc[0] * mult_ref[2, j] + back
        f1 = f1 + acc[1] * mult_ref[3, j1]
        f2 = f2 + acc[2] * mult_ref[4, j2]
        out_ref[pl.ds(j2, 1), :] = jnp.sum(f2, axis=0, keepdims=True)
        return f0, f1

    zero = jnp.zeros((8, BLOCK), F32)
    f0, f1 = lax.fori_loop(0, NBLK, main, (zero, zero), unroll=SAME_UNROLL)
    out_ref[NBLK - 1 : NBLK, :] = jnp.sum(f0, axis=0, keepdims=True)
    out_ref[NBLK - 2 : NBLK - 1, :] = jnp.sum(f1, axis=0, keepdims=True)


def adj_kernel(o_ref, up_ref, down_ref, gain_ref, pairs_ref, count_ref, out_ref, xt_ref, r_ref, mb_ref):
    out_ref[...] = gain_ref[...]

    def build(j, carry):
        for half, ref in ((0, up_ref), (1, down_ref)):
            v = ref[j]
            left, _ = forms(v)
            partner_form(v, left, j + half * EDGE, xt_ref, mb_ref)
            _, right = forms(o_ref[j + half * (NBLK - EDGE)])
            r_ref[j + half * EDGE] = right.astype(BF)
        return carry

    lax.fori_loop(0, EDGE, build, 0, unroll=2)
    count = count_ref[0, 0]

    def main(u, carry):
        found = []
        for x in range(ADJ_UNROLL):
            t = u * ADJ_UNROLL + x
            i = jnp.clip(pairs_ref[0, t], 0, NBLK - 1)
            j = jnp.clip(pairs_ref[1, t], 0, 2 * EDGE - 1)
            k = jnp.clip(jnp.where(i < EDGE, i, i - (NBLK - 2 * EDGE)), 0, 2 * EDGE - 1)
            d = jnp.dot(xt_ref[j], r_ref[k], preferred_element_type=F32)
            e = jnp.exp2(d[:, :BLOCK]) * d[:, BLOCK:] * mb_ref[j]
            found.append((i, jnp.where(t < count, jnp.sum(e, axis=0, keepdims=True), 0.0)))
        for i, e in found:
            out_ref[pl.ds(i, 1), :] += e
        return carry

    lax.fori_loop(0, (count + ADJ_UNROLL - 1) // ADJ_UNROLL, main, 0)


def gather_kernel(gain_ref, slot_ref, attr_ref, out_ref):
    turned = gain_ref[...].T
    high = rounded(turned)
    table = jnp.concatenate([high, turned - high], axis=1).astype(BF)

    def step(s, carry):
        low = pl.multiple_of(s * GCHUNK, GCHUNK)
        slot = slot_ref[:, pl.ds(low, GCHUNK)]
        block = onehot_rows(NBLK, slot >> 7).astype(BF)
        z = jnp.dot(table, jnp.concatenate([block, block], axis=0), preferred_element_type=F32)
        lane = lax.broadcasted_iota(jnp.int32, (BLOCK, GCHUNK), 0) == (slot & 127)
        gain = jnp.sum(jnp.where(lane, z, 0.0), axis=0, keepdims=True)
        out_ref[:, pl.ds(low, GCHUNK)] = attr_ref[6:7, pl.ds(low, GCHUNK)] + RATE * gain
        return carry

    lax.fori_loop(0, FLOC_DEV // GCHUNK, step, 0)


VMEM = pl.BlockSpec(memory_space=pltpu.VMEM)
SMEM = pl.BlockSpec(memory_space=pltpu.SMEM)


def call(kernel, name, out, ins, scratch, cost, *args):
    return pl.pallas_call(
        kernel,
        out_shape=out,
        in_specs=ins,
        out_specs=jax.tree.map(lambda _: VMEM, out),
        scratch_shapes=scratch,
        compiler_params=pltpu.CompilerParams(vmem_limit_bytes=52 * MIB),
        cost_estimate=pl.CostEstimate(flops=cost, bytes_accessed=2 * MIB, transcendentals=0),
        name=name,
    )(*args)


def shape(*dims):
    return jax.ShapeDtypeStruct(dims, F32)


def body(floc_attr, floc_slot, same_pairs, same_count, adj_pairs, neighbour_pair_count):
    tiles = lax.axis_size("tile")
    cap_blocks = NBLK // tiles
    segs = lax.axis_size("seg")
    slot_row = floc_slot.reshape(1, FLOC_DEV)
    send, mult = call(
        scatter_kernel,
        "scatter",
        (shape(NBLK, ATTR, BLOCK), shape(8, NBLK)),
        [VMEM, VMEM, VMEM, SMEM],
        [
            pltpu.VMEM((ATTR * BLOCK, 2 * CHUNK), BF),
            pltpu.VMEM((NBLK, 2 * CHUNK), BF),
            pltpu.VMEM((ATTR * BLOCK, NBLK), F32),
        ],
        2 * 2 * ATTR * BLOCK * NBLK * FLOC_DEV,
        floc_attr,
        slot_row,
        same_pairs.reshape(2, PSAME),
        same_count,
    )
    send = send.reshape(tiles, cap_blocks, ATTR, BLOCK)
    owned = lax.all_to_all(send, "tile", split_axis=0, concat_axis=0, tiled=True)
    owned = owned.reshape(NBLK, ATTR, BLOCK)
    up = lax.ppermute(owned[NBLK - EDGE :], "seg", [(i, i + 1) for i in range(segs - 1)])
    down = lax.ppermute(owned[:EDGE], "seg", [(i + 1, i) for i in range(segs - 1)])
    gain = call(
        same_kernel,
        "same_pairs",
        shape(NBLK, BLOCK),
        [VMEM, SMEM],
        [
            pltpu.VMEM((NBLK, BLOCK, KF), BF),
            pltpu.VMEM((NBLK + 2, KF, 2 * BLOCK), BF),
            pltpu.VMEM((NBLK, BLOCK, BLOCK), F32),
        ],
        40_000_000_000,
        owned,
        mult,
    )
    gain = call(
        adj_kernel,
        "adjacent_pairs",
        shape(NBLK, BLOCK),
        [VMEM, VMEM, VMEM, VMEM, SMEM, SMEM],
        [
            pltpu.VMEM((2 * EDGE, BLOCK, KF), BF),
            pltpu.VMEM((2 * EDGE, KF, 2 * BLOCK), BF),
            pltpu.VMEM((2 * EDGE, BLOCK, BLOCK), F32),
        ],
        10_000_000_000,
        owned,
        up,
        down,
        gain,
        adj_pairs.reshape(2, PADJ),
        neighbour_pair_count,
    )
    gain = gain.reshape(tiles, cap_blocks, BLOCK)
    returned = lax.all_to_all(gain, "tile", split_axis=0, concat_axis=0, tiled=True)
    out = call(
        gather_kernel,
        "final_gather",
        shape(1, FLOC_DEV),
        [VMEM, VMEM, VMEM],
        [],
        10_000_000_000,
        returned.reshape(NBLK, BLOCK),
        slot_row,
        floc_attr,
    )
    return out.reshape(FLOC_DEV)


def solution(mesh):
    placed = (
        P(None, ("seg", "tile")),
        P(("seg", "tile")),
        P("seg", "tile", None, None),
        P("seg", "tile"),
        P("seg", "tile", None, None),
        P("seg", "tile"),
    )
    return jax.shard_map(
        body, mesh=mesh, in_specs=placed, out_specs=P(("seg", "tile")), check_vma=False
    )
```

```python
import functools

import jax
import jax.numpy as jnp
import numpy as np
from jax import lax
from jax.experimental import pallas as pl
from jax.experimental.pallas import tpu as pltpu
from jax.sharding import PartitionSpec as P

ATTR = 8
BLOCK = 128
FLOC_DEV = 16384
NBLK = 256
EDGE = 32
RATE = 0.05
PSAME = 1024
PADJ = 128
SCALE = float(np.sqrt(np.log2(np.e)))
CHUNK = 1024
GCHUNK = 1024
KF = 48
KADJ = 64
GROUP = 16
ADJ_UNROLL = 8
QROWS = 32
MIB = 2**20
BF = jnp.bfloat16
F32 = jnp.float32


def rounded(x):
    return x.astype(BF).astype(F32)


def onehot_rows(rows, index):
    shape = (rows, index.shape[1])
    return jnp.where(lax.broadcasted_iota(jnp.int32, shape, 0) == index, 1.0, 0.0)


def scatter_kernel(attr_ref, slot_ref, pairs_ref, count_ref, out_ref, mult_ref, y_ref, b_ref, acc_ref):
    first = pairs_ref[0:1, :]
    offset = pairs_ref[1:2, :] - first + 2
    live = lax.broadcasted_iota(jnp.int32, (1, PSAME), 1) < count_ref[0, 0]
    offset = jnp.where(live, offset, -1)
    mult_ref[...] = lax.dot_general(
        onehot_rows(8, offset).astype(BF),
        onehot_rows(NBLK, first).astype(BF),
        (((1,), (1,)), ((), ())),
        preferred_element_type=F32,
    )
    row = lax.broadcasted_iota(jnp.int32, (ATTR, CHUNK), 0)

    def step(s, carry):
        low = pl.multiple_of(s * CHUNK, CHUNK)
        slot = slot_ref[:, pl.ds(low, CHUNK)]
        block = onehot_rows(NBLK, slot >> 7).astype(BF)
        b_ref[:, :CHUNK] = block
        b_ref[:, CHUNK:] = block
        lane = lax.broadcasted_iota(jnp.int32, (BLOCK, CHUNK), 0) == (slot & 127)
        value = attr_ref[:, pl.ds(low, CHUNK)]
        value = jnp.where(row < 6, value * SCALE, value)
        high = rounded(value)
        rest = value - high
        for a in range(ATTR):
            at = slice(a * BLOCK, (a + 1) * BLOCK)
            y_ref[at, :CHUNK] = jnp.where(lane, high[a : a + 1], 0.0).astype(BF)
            y_ref[at, CHUNK:] = jnp.where(lane, rest[a : a + 1], 0.0).astype(BF)
        acc_ref[...] += lax.dot_general(
            y_ref[...], b_ref[...], (((1,), (1,)), ((), ())), preferred_element_type=F32
        )
        return carry

    acc_ref[...] = jnp.zeros_like(acc_ref)
    lax.fori_loop(0, FLOC_DEV // CHUNK, step, 0)
    for a in range(ATTR):
        out_ref[:, a, :] = acc_ref[a * BLOCK : (a + 1) * BLOCK, :].T


def forms(v):
    row = lax.broadcasted_iota(jnp.int32, (8, BLOCK), 0)
    six = row < 6
    lo3 = row < 3
    high = rounded(v)
    rest = v - high
    norm = -0.5 * jnp.sum(jnp.where(six, v * v, 0.0), axis=0, keepdims=True)
    n0 = rounded(norm)
    n1 = rounded(norm - n0)
    n2 = norm - n0 - n1
    k = jnp.where(lo3, row, row - 3)
    parts = jnp.where(k == 0, n0, jnp.where(k == 1, n1, n2))
    one = jnp.where(six, 1.0, 0.0)
    h6 = jnp.where(six, high, 0.0)
    m6 = jnp.where(six, rest, 0.0)
    zero = jnp.zeros((8, BLOCK), F32)
    left = [high, rest, high, rest, jnp.where(lo3, parts, one), zero]
    right = [h6, m6, m6, h6, jnp.where(lo3, one, jnp.where(six, parts, 0.0)), zero]
    return left, right


def stacked(rows):
    return jnp.concatenate(rows, axis=0).astype(BF)


def spread_form():
    row = lax.broadcasted_iota(jnp.int32, (KF, 2 * BLOCK), 0)
    lane = lax.broadcasted_iota(jnp.int32, (KF, 2 * BLOCK), 1)
    want = jnp.where(lane < BLOCK, 6, 7)
    return jnp.where((row == want) | (row == want + 8), 1.0, 0.0).astype(BF)


def same_kernel(o_ref, mult_ref, out_ref, xt0, xt1, r0, r1):
    spread = spread_form()
    shape8 = (8, BLOCK)
    diff = lax.broadcasted_iota(jnp.int32, shape8, 1) - lax.broadcasted_iota(jnp.int32, shape8, 0)

    def build(j, x, xt_ref, r_ref):
        left, right = forms(o_ref[j])
        r_ref[x + 2] = stacked(right)
        xt_ref[x] = stacked(left).T

    def main(j, x, xt_ref, r_ref, carry):
        f1, f2 = carry
        j1 = jnp.maximum(j - 1, 0)
        j2 = jnp.maximum(j - 2, 0)
        own = [o_ref[j], o_ref[j1], o_ref[j2]]
        radius = [jnp.broadcast_to(o[7:8], shape8) for o in own]
        mass1 = own[1][6:7] * mult_ref[1, j]
        mass2 = own[2][6:7] * mult_ref[0, j]
        rhs = jnp.concatenate([r_ref[x + 2], r_ref[x + 1], r_ref[x], spread], axis=1)
        acc = [jnp.zeros(shape8, F32) for _ in range(3)]
        rev = []
        for q in range(0, BLOCK, QROWS):
            d = jnp.dot(xt_ref[x, q : q + QROWS, :], rhs, preferred_element_type=F32)
            for s in range(0, QROWS, 8):
                z = d[s : s + 8]
                mass = z[:, 3 * BLOCK : 4 * BLOCK]
                reach = z[:, 4 * BLOCK : 5 * BLOCK]
                w = []
                for a in range(3):
                    t = reach + radius[a]
                    e = jnp.exp2(z[:, a * BLOCK : (a + 1) * BLOCK]) * (t * t)
                    if a == 0:
                        e = jnp.where(diff == q + s, 0.0, e)
                    w.append(e)
                    acc[a] = acc[a] + e * mass
                rev.append(w[1] * mass1 + w[2] * mass2)
        back = jnp.sum(jnp.concatenate(rev, axis=0).T.reshape(BLOCK // 8, 8, BLOCK), axis=0)
        f0 = acc[0] * mult_ref[2, j] + back
        f1 = f1 + acc[1] * mult_ref[3, j1]
        f2 = f2 + acc[2] * mult_ref[4, j2]
        out_ref[pl.ds(j2, 1), :] = jnp.sum(f2, axis=0, keepdims=True)
        return f0, f1

    r0[0] = jnp.zeros((KF, BLOCK), BF)
    r0[1] = jnp.zeros((KF, BLOCK), BF)
    for x in range(GROUP):
        build(x, x, xt0, r0)

    def groups(u, carry):
        for half, (xa, ra, xb, rb) in enumerate(((xt0, r0, xt1, r1), (xt1, r1, xt0, r0))):
            base = (2 * u + half) * GROUP
            later = jnp.minimum(base + GROUP, NBLK - GROUP)
            rb[0] = ra[GROUP]
            rb[1] = ra[GROUP + 1]
            for x in range(GROUP):
                build(later + x, x, xb, rb)
                carry = main(base + x, x, xa, ra, carry)
        return carry

    zero = jnp.zeros(shape8, F32)
    f0, f1 = lax.fori_loop(0, NBLK // (2 * GROUP), groups, (zero, zero))
    out_ref[NBLK - 1 : NBLK, :] = jnp.sum(f0, axis=0, keepdims=True)
    out_ref[NBLK - 2 : NBLK - 1, :] = jnp.sum(f1, axis=0, keepdims=True)


def two(x):
    high = rounded(x)
    return high, x - high


def adj_left(v):
    left, _ = forms(v)
    row = lax.broadcasted_iota(jnp.int32, (8, BLOCK), 0)
    mass = v[6:7]
    radius = v[7:8]
    x = jnp.where(row < 4, mass, jnp.where(row < 8, mass * radius, 0.0))
    h, m = two(x)
    first = jnp.where(row % 4 < 2, h, m)
    h, m = two(jnp.where(row < 4, mass * radius * radius, 0.0))
    second = jnp.where(row % 4 < 2, h, m)
    zero = jnp.zeros((8, BLOCK), F32)
    return stacked(left[:5] + [first, second, zero])


def adj_right(v):
    _, right = forms(v)
    row = lax.broadcasted_iota(jnp.int32, (8, BLOCK), 0)
    radius = v[7:8]
    h, m = two(jnp.where(row < 4, radius * radius, 2.0 * radius))
    first = jnp.where(row % 2 == 0, h, m)
    second = jnp.where((row < 4) & (row % 2 == 0), 1.0, 0.0)
    zero = jnp.zeros((8, BLOCK), F32)
    arg = right[:5] + [zero, zero, zero]
    reach = [zero] * 5 + [first, second, zero]
    return jnp.concatenate([stacked(arg), stacked(reach)], axis=1)


def adj_kernel(o_ref, up_ref, down_ref, gain_ref, pairs_ref, list_ref, count_ref, out_ref, xt_ref, r_ref, found_ref):
    def build(j, carry):
        for half, ref in ((0, up_ref), (1, down_ref)):
            xt_ref[j + half * EDGE] = adj_left(ref[j]).T
            r_ref[j + half * EDGE] = adj_right(o_ref[j + half * (NBLK - EDGE)])
        return carry

    lax.fori_loop(0, EDGE, build, 0, unroll=8)
    count = count_ref[0, 0]
    found_ref[...] = jnp.zeros_like(found_ref)

    def main(u, carry):
        for x in range(ADJ_UNROLL):
            t = u * ADJ_UNROLL + x
            i = pairs_ref[0, t]
            j = jnp.clip(pairs_ref[1, t], 0, 2 * EDGE - 1)
            k = jnp.clip(jnp.where(i < EDGE, i, i - (NBLK - 2 * EDGE)), 0, 2 * EDGE - 1)
            d = jnp.dot(xt_ref[j], r_ref[k], preferred_element_type=F32)
            e = jnp.exp2(d[:, :BLOCK]) * d[:, BLOCK:]
            found_ref[pl.ds(t, 1), :] = jnp.sum(e, axis=0, keepdims=True)
        return carry

    lax.fori_loop(0, (count + ADJ_UNROLL - 1) // ADJ_UNROLL, main, 0)
    live = lax.broadcasted_iota(jnp.int32, (1, PADJ), 1) < count
    owner = onehot_rows(NBLK, jnp.where(live, list_ref[0:1, :], -1)).astype(BF)
    h, m = two(found_ref[...])
    h2, m2 = two(m)
    total = gain_ref[...]
    for part in (m2, h2, h):
        total = total + jnp.dot(owner, part.astype(BF), preferred_element_type=F32)
    out_ref[...] = total


def gather_kernel(gain_ref, slot_ref, attr_ref, out_ref):
    turned = gain_ref[...].T
    high, rest = two(turned)
    table = jnp.concatenate([high, rest], axis=1).astype(BF)
    number = lax.broadcasted_iota(jnp.int32, (NBLK, GCHUNK), 0).astype(F32).astype(BF)

    def step(s, carry):
        low = pl.multiple_of(s * GCHUNK, GCHUNK)
        slot = slot_ref[:, pl.ds(low, GCHUNK)]
        block = number == (slot >> 7).astype(F32).astype(BF)
        block = jnp.where(block, jnp.ones((), BF), jnp.zeros((), BF))
        z = jnp.dot(table, jnp.concatenate([block, block], axis=0), preferred_element_type=F32)
        lane = lax.broadcasted_iota(jnp.int32, (BLOCK, GCHUNK), 0) == (slot & 127)
        gain = jnp.sum(jnp.where(lane, z, 0.0), axis=0, keepdims=True)
        out_ref[:, pl.ds(low, GCHUNK)] = attr_ref[6:7, pl.ds(low, GCHUNK)] + RATE * gain
        return carry

    lax.fori_loop(0, FLOC_DEV // GCHUNK, step, 0, unroll=2)


VMEM = pl.BlockSpec(memory_space=pltpu.VMEM)
SMEM = pl.BlockSpec(memory_space=pltpu.SMEM)


def call(kernel, name, out, ins, scratch, cost, *args):
    return pl.pallas_call(
        kernel,
        out_shape=out,
        in_specs=ins,
        out_specs=jax.tree.map(lambda _: VMEM, out),
        scratch_shapes=scratch,
        compiler_params=pltpu.CompilerParams(vmem_limit_bytes=52 * MIB),
        cost_estimate=pl.CostEstimate(flops=cost, bytes_accessed=2 * MIB, transcendentals=0),
        name=name,
    )(*args)


def shape(*dims):
    return jax.ShapeDtypeStruct(dims, F32)


def body(floc_attr, floc_slot, same_pairs, same_count, adj_pairs, neighbour_pair_count):
    tiles = lax.axis_size("tile")
    cap_blocks = NBLK // tiles
    segs = lax.axis_size("seg")
    slot_row = floc_slot.reshape(1, FLOC_DEV)
    send, mult = call(
        scatter_kernel,
        "scatter",
        (shape(NBLK, ATTR, BLOCK), shape(8, NBLK)),
        [VMEM, VMEM, VMEM, SMEM],
        [
            pltpu.VMEM((ATTR * BLOCK, 2 * CHUNK), BF),
            pltpu.VMEM((NBLK, 2 * CHUNK), BF),
            pltpu.VMEM((ATTR * BLOCK, NBLK), F32),
        ],
        2 * 2 * ATTR * BLOCK * NBLK * FLOC_DEV,
        floc_attr,
        slot_row,
        same_pairs.reshape(2, PSAME),
        same_count,
    )
    send = send.reshape(tiles, cap_blocks, ATTR, BLOCK)
    owned = lax.all_to_all(send, "tile", split_axis=0, concat_axis=0, tiled=True)
    owned = owned.reshape(NBLK, ATTR, BLOCK)
    up = lax.ppermute(owned[NBLK - EDGE :], "seg", [(i, i + 1) for i in range(segs - 1)])
    down = lax.ppermute(owned[:EDGE], "seg", [(i + 1, i) for i in range(segs - 1)])
    gain = call(
        same_kernel,
        "same_pairs",
        shape(NBLK, BLOCK),
        [VMEM, SMEM],
        [
            pltpu.VMEM((GROUP, BLOCK, KF), BF),
            pltpu.VMEM((GROUP, BLOCK, KF), BF),
            pltpu.VMEM((GROUP + 2, KF, BLOCK), BF),
            pltpu.VMEM((GROUP + 2, KF, BLOCK), BF),
        ],
        40_000_000_000,
        owned,
        mult,
    )
    gain = call(
        adj_kernel,
        "adjacent_pairs",
        shape(NBLK, BLOCK),
        [VMEM, VMEM, VMEM, VMEM, SMEM, VMEM, SMEM],
        [
            pltpu.VMEM((2 * EDGE, BLOCK, KADJ), BF),
            pltpu.VMEM((2 * EDGE, KADJ, 2 * BLOCK), BF),
            pltpu.VMEM((PADJ, BLOCK), F32),
        ],
        10_000_000_000,
        owned,
        up,
        down,
        gain,
        adj_pairs.reshape(2, PADJ),
        adj_pairs.reshape(2, PADJ),
        neighbour_pair_count,
    )
    gain = gain.reshape(tiles, cap_blocks, BLOCK)
    returned = lax.all_to_all(gain, "tile", split_axis=0, concat_axis=0, tiled=True)
    out = call(
        gather_kernel,
        "final_gather",
        shape(1, FLOC_DEV),
        [VMEM, VMEM, VMEM],
        [],
        10_000_000_000,
        returned.reshape(NBLK, BLOCK),
        slot_row,
        floc_attr,
    )
    return out.reshape(FLOC_DEV)


def solution(mesh):
    placed = (
        P(None, ("seg", "tile")),
        P(("seg", "tile")),
        P("seg", "tile", None, None),
        P("seg", "tile"),
        P("seg", "tile", None, None),
        P("seg", "tile"),
    )
    return jax.shard_map(
        body, mesh=mesh, in_specs=placed, out_specs=P(("seg", "tile")), check_vma=False
    )
```

```python
import functools

import jax
import jax.numpy as jnp
import numpy as np
from jax import lax
from jax.experimental import pallas as pl
from jax.experimental.pallas import tpu as pltpu
from jax.sharding import PartitionSpec as P

ATTR = 8
BLOCK = 128
FLOC_DEV = 16384
NBLK = 256
EDGE = 32
RATE = 0.05
PSAME = 1024
PADJ = 128
SCALE = float(np.sqrt(np.log2(np.e)))
CHUNK = 1024
GCHUNK = 1024
KF = 48
KADJ = 64
GROUP = 16
ADJ_UNROLL = 32
QROWS = 32
MIB = 2**20
BF = jnp.bfloat16
F32 = jnp.float32


def rounded(x):
    return x.astype(BF).astype(F32)


def onehot_rows(rows, index):
    shape = (rows, index.shape[1])
    return jnp.where(lax.broadcasted_iota(jnp.int32, shape, 0) == index, 1.0, 0.0)


def fetch(sources, targets, sems):
    copies = [
        pltpu.make_async_copy(source, target, sems.at[n])
        for n, (source, target) in enumerate(zip(sources, targets))
    ]
    for copy in copies:
        copy.start()
    return copies


def scatter_kernel(attr_hbm, slot_hbm, pairs_hbm, count_ref, out_ref, mult_ref, attr_ref, slot_ref, pairs_ref, sems, y_ref, b_ref, acc_ref):
    copies = fetch((attr_hbm, slot_hbm, pairs_hbm), (attr_ref, slot_ref, pairs_ref), sems)
    acc_ref[...] = jnp.zeros_like(acc_ref)
    copies[2].wait()
    first = pairs_ref[0:1, :]
    offset = pairs_ref[1:2, :] - first + 2
    live = lax.broadcasted_iota(jnp.int32, (1, PSAME), 1) < count_ref[0, 0]
    offset = jnp.where(live, offset, -1)
    mult_ref[...] = lax.dot_general(
        onehot_rows(8, offset).astype(BF),
        onehot_rows(NBLK, first).astype(BF),
        (((1,), (1,)), ((), ())),
        preferred_element_type=F32,
    )
    row = lax.broadcasted_iota(jnp.int32, (ATTR, CHUNK), 0)

    def step(s, carry):
        low = pl.multiple_of(s * CHUNK, CHUNK)
        slot = slot_ref[:, pl.ds(low, CHUNK)]
        block = onehot_rows(NBLK, slot >> 7).astype(BF)
        b_ref[:, :CHUNK] = block
        b_ref[:, CHUNK:] = block
        lane = lax.broadcasted_iota(jnp.int32, (BLOCK, CHUNK), 0) == (slot & 127)
        value = attr_ref[:, pl.ds(low, CHUNK)]
        value = jnp.where(row < 6, value * SCALE, value)
        high = rounded(value)
        rest = value - high
        for a in range(ATTR):
            at = slice(a * BLOCK, (a + 1) * BLOCK)
            y_ref[at, :CHUNK] = jnp.where(lane, high[a : a + 1], 0.0).astype(BF)
            y_ref[at, CHUNK:] = jnp.where(lane, rest[a : a + 1], 0.0).astype(BF)
        acc_ref[...] += lax.dot_general(
            y_ref[...], b_ref[...], (((1,), (1,)), ((), ())), preferred_element_type=F32
        )
        return carry

    copies[0].wait()
    copies[1].wait()
    lax.fori_loop(0, FLOC_DEV // CHUNK, step, 0)
    for a in range(ATTR):
        out_ref[:, a, :] = acc_ref[a * BLOCK : (a + 1) * BLOCK, :].T


def forms(v):
    row = lax.broadcasted_iota(jnp.int32, (8, BLOCK), 0)
    six = row < 6
    lo3 = row < 3
    high = rounded(v)
    rest = v - high
    norm = -0.5 * jnp.sum(jnp.where(six, v * v, 0.0), axis=0, keepdims=True)
    n0 = rounded(norm)
    n1 = rounded(norm - n0)
    n2 = norm - n0 - n1
    k = jnp.where(lo3, row, row - 3)
    parts = jnp.where(k == 0, n0, jnp.where(k == 1, n1, n2))
    one = jnp.where(six, 1.0, 0.0)
    h6 = jnp.where(six, high, 0.0)
    m6 = jnp.where(six, rest, 0.0)
    zero = jnp.zeros((8, BLOCK), F32)
    left = [high, rest, high, rest, jnp.where(lo3, parts, one), zero]
    right = [h6, m6, m6, h6, jnp.where(lo3, one, jnp.where(six, parts, 0.0)), zero]
    return left, right


def stacked(rows):
    return jnp.concatenate(rows, axis=0).astype(BF)


def spread_form():
    row = lax.broadcasted_iota(jnp.int32, (KF, 2 * BLOCK), 0)
    lane = lax.broadcasted_iota(jnp.int32, (KF, 2 * BLOCK), 1)
    want = jnp.where(lane < BLOCK, 6, 7)
    return jnp.where((row == want) | (row == want + 8), 1.0, 0.0).astype(BF)


def same_kernel(o_ref, mult_ref, out_ref, xt0, xt1, r0, r1):
    spread = spread_form()
    shape8 = (8, BLOCK)
    diff = lax.broadcasted_iota(jnp.int32, shape8, 1) - lax.broadcasted_iota(jnp.int32, shape8, 0)

    def build(j, x, xt_ref, r_ref):
        left, right = forms(o_ref[j])
        r_ref[x + 2] = stacked(right)
        xt_ref[x] = stacked(left).T

    def main(j, x, xt_ref, r_ref, carry):
        f1, f2 = carry
        j1 = jnp.maximum(j - 1, 0)
        j2 = jnp.maximum(j - 2, 0)
        own = [o_ref[j], o_ref[j1], o_ref[j2]]
        radius = [jnp.broadcast_to(o[7:8], shape8) for o in own]
        mass1 = own[1][6:7] * mult_ref[1, j]
        mass2 = own[2][6:7] * mult_ref[0, j]
        rhs = jnp.concatenate([r_ref[x + 2], r_ref[x + 1], r_ref[x], spread], axis=1)
        acc = [jnp.zeros(shape8, F32) for _ in range(3)]
        rev = []
        for q in range(0, BLOCK, QROWS):
            d = jnp.dot(xt_ref[x, q : q + QROWS, :], rhs, preferred_element_type=F32)
            for s in range(0, QROWS, 8):
                z = d[s : s + 8]
                mass = z[:, 3 * BLOCK : 4 * BLOCK]
                reach = z[:, 4 * BLOCK : 5 * BLOCK]
                w = []
                for a in range(3):
                    t = reach + radius[a]
                    e = jnp.exp2(z[:, a * BLOCK : (a + 1) * BLOCK]) * (t * t)
                    if a == 0:
                        e = jnp.where(diff == q + s, 0.0, e)
                    w.append(e)
                    acc[a] = acc[a] + e * mass
                rev.append(w[1] * mass1 + w[2] * mass2)
        back = jnp.sum(jnp.concatenate(rev, axis=0).T.reshape(BLOCK // 8, 8, BLOCK), axis=0)
        f0 = acc[0] * mult_ref[2, j] + back
        f1 = f1 + acc[1] * mult_ref[3, j1]
        f2 = f2 + acc[2] * mult_ref[4, j2]
        out_ref[pl.ds(j2, 1), :] = jnp.sum(f2, axis=0, keepdims=True)
        return f0, f1

    r0[0] = jnp.zeros((KF, BLOCK), BF)
    r0[1] = jnp.zeros((KF, BLOCK), BF)
    for x in range(GROUP):
        build(x, x, xt0, r0)

    def groups(u, carry):
        for half, (xa, ra, xb, rb) in enumerate(((xt0, r0, xt1, r1), (xt1, r1, xt0, r0))):
            base = (2 * u + half) * GROUP
            later = jnp.minimum(base + GROUP, NBLK - GROUP)
            rb[0] = ra[GROUP]
            rb[1] = ra[GROUP + 1]
            for x in range(GROUP):
                build(later + x, x, xb, rb)
                carry = main(base + x, x, xa, ra, carry)
        return carry

    zero = jnp.zeros(shape8, F32)
    f0, f1 = lax.fori_loop(0, NBLK // (2 * GROUP), groups, (zero, zero))
    out_ref[NBLK - 1 : NBLK, :] = jnp.sum(f0, axis=0, keepdims=True)
    out_ref[NBLK - 2 : NBLK - 1, :] = jnp.sum(f1, axis=0, keepdims=True)


def two(x):
    high = rounded(x)
    return high, x - high


def adj_left(v):
    left, _ = forms(v)
    row = lax.broadcasted_iota(jnp.int32, (8, BLOCK), 0)
    mass = v[6:7]
    radius = v[7:8]
    x = jnp.where(row < 4, mass, jnp.where(row < 8, mass * radius, 0.0))
    h, m = two(x)
    first = jnp.where(row % 4 < 2, h, m)
    h, m = two(jnp.where(row < 4, mass * radius * radius, 0.0))
    second = jnp.where(row % 4 < 2, h, m)
    zero = jnp.zeros((8, BLOCK), F32)
    return stacked(left[:5] + [first, second, zero])


def adj_right(v):
    _, right = forms(v)
    row = lax.broadcasted_iota(jnp.int32, (8, BLOCK), 0)
    radius = v[7:8]
    h, m = two(jnp.where(row < 4, radius * radius, 2.0 * radius))
    first = jnp.where(row % 2 == 0, h, m)
    second = jnp.where((row < 4) & (row % 2 == 0), 1.0, 0.0)
    zero = jnp.zeros((8, BLOCK), F32)
    arg = right[:5] + [zero, zero, zero]
    reach = [zero] * 5 + [first, second, zero]
    return jnp.concatenate([stacked(arg), stacked(reach)], axis=1)


def adj_kernel(o_ref, up_ref, down_ref, gain_ref, pairs_ref, list_ref, count_ref, out_ref, xt_ref, r_ref, found_ref):
    def build(j, carry):
        for half, ref in ((0, up_ref), (1, down_ref)):
            xt_ref[j + half * EDGE] = adj_left(ref[j]).T
            r_ref[j + half * EDGE] = adj_right(o_ref[j + half * (NBLK - EDGE)])
        return carry

    lax.fori_loop(0, EDGE, build, 0, unroll=8)
    count = count_ref[0, 0]
    found_ref[...] = jnp.zeros_like(found_ref)

    def main(u, carry):
        for x in range(ADJ_UNROLL):
            t = u * ADJ_UNROLL + x
            i = pairs_ref[0, t]
            j = jnp.clip(pairs_ref[1, t], 0, 2 * EDGE - 1)
            k = jnp.clip(jnp.where(i < EDGE, i, i - (NBLK - 2 * EDGE)), 0, 2 * EDGE - 1)
            d = jnp.dot(xt_ref[j], r_ref[k], preferred_element_type=F32)
            e = jnp.exp2(d[:, :BLOCK]) * d[:, BLOCK:]
            found_ref[pl.ds(t, 1), :] = jnp.sum(e, axis=0, keepdims=True)
        return carry

    lax.fori_loop(0, (count + ADJ_UNROLL - 1) // ADJ_UNROLL, main, 0)
    live = lax.broadcasted_iota(jnp.int32, (1, PADJ), 1) < count
    owner = onehot_rows(NBLK, jnp.where(live, list_ref[0:1, :], -1)).astype(BF)
    h, m = two(found_ref[...])
    h2, m2 = two(m)
    total = gain_ref[...]
    for part in (m2, h2, h):
        total = total + jnp.dot(owner, part.astype(BF), preferred_element_type=F32)
    out_ref[...] = total


def gather_kernel(gain_ref, slot_ref, attr_ref, out_ref):
    turned = gain_ref[...].T
    high, rest = two(turned)
    table = jnp.concatenate([high, rest], axis=1).astype(BF)
    number = lax.broadcasted_iota(jnp.int32, (NBLK, GCHUNK), 0).astype(F32).astype(BF)

    def step(s, carry):
        low = pl.multiple_of(s * GCHUNK, GCHUNK)
        slot = slot_ref[:, pl.ds(low, GCHUNK)]
        block = number == (slot >> 7).astype(F32).astype(BF)
        block = jnp.where(block, jnp.ones((), BF), jnp.zeros((), BF))
        z = jnp.dot(table, jnp.concatenate([block, block], axis=0), preferred_element_type=F32)
        lane = lax.broadcasted_iota(jnp.int32, (BLOCK, GCHUNK), 0) == (slot & 127)
        gain = jnp.sum(jnp.where(lane, z, 0.0), axis=0, keepdims=True)
        out_ref[:, pl.ds(low, GCHUNK)] = attr_ref[6:7, pl.ds(low, GCHUNK)] + RATE * gain
        return carry

    lax.fori_loop(0, FLOC_DEV // GCHUNK, step, 0, unroll=2)


VMEM = pl.BlockSpec(memory_space=pltpu.VMEM)
SMEM = pl.BlockSpec(memory_space=pltpu.SMEM)
HBM = pl.BlockSpec(memory_space=pltpu.HBM)


def call(kernel, name, out, ins, scratch, cost, *args):
    return pl.pallas_call(
        kernel,
        out_shape=out,
        in_specs=ins,
        out_specs=jax.tree.map(lambda _: VMEM, out),
        scratch_shapes=scratch,
        compiler_params=pltpu.CompilerParams(vmem_limit_bytes=(60 if name == "scatter" else 52) * MIB),
        cost_estimate=pl.CostEstimate(flops=cost, bytes_accessed=2 * MIB, transcendentals=0),
        name=name,
    )(*args)


def shape(*dims):
    return jax.ShapeDtypeStruct(dims, F32)


def body(floc_attr, floc_slot, same_pairs, same_count, adj_pairs, neighbour_pair_count):
    tiles = lax.axis_size("tile")
    cap_blocks = NBLK // tiles
    segs = lax.axis_size("seg")
    slot_row = floc_slot.reshape(1, FLOC_DEV)
    send, mult = call(
        scatter_kernel,
        "scatter",
        (shape(NBLK, ATTR, BLOCK), shape(8, NBLK)),
        [HBM, HBM, HBM, SMEM],
        [
            pltpu.VMEM((ATTR, FLOC_DEV), F32),
            pltpu.VMEM((1, FLOC_DEV), jnp.int32),
            pltpu.VMEM((2, PSAME), jnp.int32),
            pltpu.SemaphoreType.DMA((3,)),
            pltpu.VMEM((ATTR * BLOCK, 2 * CHUNK), BF),
            pltpu.VMEM((NBLK, 2 * CHUNK), BF),
            pltpu.VMEM((ATTR * BLOCK, NBLK), F32),
        ],
        2 * 2 * ATTR * BLOCK * NBLK * FLOC_DEV,
        floc_attr,
        slot_row,
        same_pairs.reshape(2, PSAME),
        same_count,
    )
    send = send.reshape(tiles, cap_blocks, ATTR, BLOCK)
    owned = lax.all_to_all(send, "tile", split_axis=0, concat_axis=0, tiled=True)
    owned = owned.reshape(NBLK, ATTR, BLOCK)
    up = lax.ppermute(owned[NBLK - EDGE :], "seg", [(i, i + 1) for i in range(segs - 1)])
    down = lax.ppermute(owned[:EDGE], "seg", [(i + 1, i) for i in range(segs - 1)])
    gain = call(
        same_kernel,
        "same_pairs",
        shape(NBLK, BLOCK),
        [VMEM, SMEM],
        [
            pltpu.VMEM((GROUP, BLOCK, KF), BF),
            pltpu.VMEM((GROUP, BLOCK, KF), BF),
            pltpu.VMEM((GROUP + 2, KF, BLOCK), BF),
            pltpu.VMEM((GROUP + 2, KF, BLOCK), BF),
        ],
        40_000_000_000,
        owned,
        mult,
    )
    gain = call(
        adj_kernel,
        "adjacent_pairs",
        shape(NBLK, BLOCK),
        [VMEM, VMEM, VMEM, VMEM, SMEM, VMEM, SMEM],
        [
            pltpu.VMEM((2 * EDGE, BLOCK, KADJ), BF),
            pltpu.VMEM((2 * EDGE, KADJ, 2 * BLOCK), BF),
            pltpu.VMEM((PADJ, BLOCK), F32),
        ],
        10_000_000_000,
        owned,
        up,
        down,
        gain,
        adj_pairs.reshape(2, PADJ),
        adj_pairs.reshape(2, PADJ),
        neighbour_pair_count,
    )
    gain = gain.reshape(tiles, cap_blocks, BLOCK)
    returned = lax.all_to_all(gain, "tile", split_axis=0, concat_axis=0, tiled=True)
    out = call(
        gather_kernel,
        "final_gather",
        shape(1, FLOC_DEV),
        [VMEM, VMEM, VMEM],
        [],
        10_000_000_000,
        returned.reshape(NBLK, BLOCK),
        slot_row,
        floc_attr,
    )
    return out.reshape(FLOC_DEV)


def solution(mesh):
    placed = (
        P(None, ("seg", "tile")),
        P(("seg", "tile")),
        P("seg", "tile", None, None),
        P("seg", "tile"),
        P("seg", "tile", None, None),
        P("seg", "tile"),
    )
    return jax.shard_map(
        body, mesh=mesh, in_specs=placed, out_specs=P(("seg", "tile")), check_vma=False
    )
```

```python
import functools

import jax
import jax.numpy as jnp
import numpy as np
from jax import lax
from jax.experimental import pallas as pl
from jax.experimental.pallas import tpu as pltpu
from jax.sharding import PartitionSpec as P

ATTR = 8
BLOCK = 128
FLOC_DEV = 16384
NBLK = 256
EDGE = 32
RATE = 0.05
PSAME = 1024
PADJ = 128
SCALE = float(np.sqrt(np.log2(np.e)))
CHUNK = 2048
GCHUNK = 1024
KF = 48
KADJ = 64
GROUP = 16
ADJ_UNROLL = 32
QROWS = 32
MIB = 2**20
BF = jnp.bfloat16
F32 = jnp.float32


def rounded(x):
    return x.astype(BF).astype(F32)


def onehot_rows(rows, index):
    shape = (rows, index.shape[1])
    return jnp.where(lax.broadcasted_iota(jnp.int32, shape, 0) == index, 1.0, 0.0)


def fetch(sources, targets, sems):
    copies = [
        pltpu.make_async_copy(source, target, sems.at[n])
        for n, (source, target) in enumerate(zip(sources, targets))
    ]
    for copy in copies:
        copy.start()
    return copies


def scatter_kernel(
    attr_hbm, slot_hbm, pairs_hbm, adj_hbm, count_ref, out_ref, mult_ref, adj_ref,
    attr_ref, slot_ref, pairs_ref, sems, y0, y1, b0, b1, acc_ref,
):
    copies = fetch(
        (attr_hbm, slot_hbm, pairs_hbm, adj_hbm), (attr_ref, slot_ref, pairs_ref, adj_ref), sems
    )
    acc_ref[...] = jnp.zeros_like(acc_ref)
    copies[2].wait()
    first = pairs_ref[0:1, :]
    offset = pairs_ref[1:2, :] - first + 2
    live = lax.broadcasted_iota(jnp.int32, (1, PSAME), 1) < count_ref[0, 0]
    offset = jnp.where(live, offset, -1)
    mult_ref[...] = lax.dot_general(
        onehot_rows(8, offset).astype(BF),
        onehot_rows(NBLK, first).astype(BF),
        (((1,), (1,)), ((), ())),
        preferred_element_type=F32,
    )
    number = lax.broadcasted_iota(jnp.int32, (NBLK, CHUNK), 0).astype(F32).astype(BF)
    row = lax.broadcasted_iota(jnp.int32, (ATTR, CHUNK), 0)
    zero = jnp.zeros((), BF)
    chunks = FLOC_DEV // CHUNK

    def spread(s, y_ref, b_ref):
        low = pl.multiple_of(s * CHUNK, CHUNK)
        slot = slot_ref[:, pl.ds(low, CHUNK)]
        block = jnp.where(number == (slot >> 7).astype(F32).astype(BF), jnp.ones((), BF), zero)
        b_ref[:, :CHUNK] = block
        b_ref[:, CHUNK:] = block
        lane = number[:BLOCK] == (slot & 127).astype(F32).astype(BF)
        value = attr_ref[:, pl.ds(low, CHUNK)]
        value = jnp.where(row < 6, value * SCALE, value)
        high = value.astype(BF)
        rest = (value - high.astype(F32)).astype(BF)
        for a in range(ATTR):
            at = slice(a * BLOCK, (a + 1) * BLOCK)
            y_ref[at, :CHUNK] = jnp.where(lane, high[a : a + 1], zero)
            y_ref[at, CHUNK:] = jnp.where(lane, rest[a : a + 1], zero)

    def place(y_ref, b_ref):
        acc_ref[...] += lax.dot_general(
            y_ref[...], b_ref[...], (((1,), (1,)), ((), ())), preferred_element_type=F32
        )

    def step(u, carry):
        spread(2 * u + 1, y1, b1)
        place(y0, b0)
        spread(jnp.minimum(2 * u + 2, chunks - 1), y0, b0)
        place(y1, b1)
        return carry

    for n in (0, 1, 3):
        copies[n].wait()
    spread(0, y0, b0)
    lax.fori_loop(0, chunks // 2, step, 0)
    for a in range(ATTR):
        out_ref[:, a, :] = acc_ref[a * BLOCK : (a + 1) * BLOCK, :].T


def forms(v):
    row = lax.broadcasted_iota(jnp.int32, (8, BLOCK), 0)
    six = row < 6
    lo3 = row < 3
    high = rounded(v)
    rest = v - high
    norm = -0.5 * jnp.sum(jnp.where(six, v * v, 0.0), axis=0, keepdims=True)
    n0 = rounded(norm)
    n1 = rounded(norm - n0)
    n2 = norm - n0 - n1
    k = jnp.where(lo3, row, row - 3)
    parts = jnp.where(k == 0, n0, jnp.where(k == 1, n1, n2))
    one = jnp.where(six, 1.0, 0.0)
    h6 = jnp.where(six, high, 0.0)
    m6 = jnp.where(six, rest, 0.0)
    zero = jnp.zeros((8, BLOCK), F32)
    left = [high, rest, high, rest, jnp.where(lo3, parts, one), zero]
    right = [h6, m6, m6, h6, jnp.where(lo3, one, jnp.where(six, parts, 0.0)), zero]
    return left, right


def stacked(rows):
    return jnp.concatenate(rows, axis=0).astype(BF)


def spread_form():
    row = lax.broadcasted_iota(jnp.int32, (KF, 2 * BLOCK), 0)
    lane = lax.broadcasted_iota(jnp.int32, (KF, 2 * BLOCK), 1)
    want = jnp.where(lane < BLOCK, 6, 7)
    return jnp.where((row == want) | (row == want + 8), 1.0, 0.0).astype(BF)


def same_kernel(o_ref, mult_ref, out_ref, xt0, xt1, r0, r1):
    spread = spread_form()
    shape8 = (8, BLOCK)
    diff = lax.broadcasted_iota(jnp.int32, shape8, 1) - lax.broadcasted_iota(jnp.int32, shape8, 0)

    def build(j, x, xt_ref, r_ref):
        left, right = forms(o_ref[j])
        r_ref[x + 2] = stacked(right)
        xt_ref[x] = stacked(left).T

    def main(j, x, xt_ref, r_ref, carry):
        f1, f2 = carry
        j1 = jnp.maximum(j - 1, 0)
        j2 = jnp.maximum(j - 2, 0)
        own = [o_ref[j], o_ref[j1], o_ref[j2]]
        radius = [jnp.broadcast_to(o[7:8], shape8) for o in own]
        mass1 = own[1][6:7] * mult_ref[1, j]
        mass2 = own[2][6:7] * mult_ref[0, j]
        rhs = jnp.concatenate([r_ref[x + 2], r_ref[x + 1], r_ref[x], spread], axis=1)
        acc = [jnp.zeros(shape8, F32) for _ in range(3)]
        rev = []
        for q in range(0, BLOCK, QROWS):
            d = jnp.dot(xt_ref[x, q : q + QROWS, :], rhs, preferred_element_type=F32)
            for s in range(0, QROWS, 8):
                z = d[s : s + 8]
                mass = z[:, 3 * BLOCK : 4 * BLOCK]
                reach = z[:, 4 * BLOCK : 5 * BLOCK]
                w = []
                for a in range(3):
                    t = reach + radius[a]
                    e = jnp.exp2(z[:, a * BLOCK : (a + 1) * BLOCK]) * (t * t)
                    if a == 0:
                        e = jnp.where(diff == q + s, 0.0, e)
                    w.append(e)
                    acc[a] = acc[a] + e * mass
                rev.append(w[1] * mass1 + w[2] * mass2)
        back = jnp.sum(jnp.concatenate(rev, axis=0).T.reshape(BLOCK // 8, 8, BLOCK), axis=0)
        f0 = acc[0] * mult_ref[2, j] + back
        f1 = f1 + acc[1] * mult_ref[3, j1]
        f2 = f2 + acc[2] * mult_ref[4, j2]
        out_ref[pl.ds(j2, 1), :] = jnp.sum(f2, axis=0, keepdims=True)
        return f0, f1

    r0[0] = jnp.zeros((KF, BLOCK), BF)
    r0[1] = jnp.zeros((KF, BLOCK), BF)
    for x in range(GROUP):
        build(x, x, xt0, r0)

    def groups(u, carry):
        for half, (xa, ra, xb, rb) in enumerate(((xt0, r0, xt1, r1), (xt1, r1, xt0, r0))):
            base = (2 * u + half) * GROUP
            later = jnp.minimum(base + GROUP, NBLK - GROUP)
            rb[0] = ra[GROUP]
            rb[1] = ra[GROUP + 1]
            for x in range(GROUP):
                build(later + x, x, xb, rb)
                carry = main(base + x, x, xa, ra, carry)
        return carry

    zero = jnp.zeros(shape8, F32)
    f0, f1 = lax.fori_loop(0, NBLK // (2 * GROUP), groups, (zero, zero))
    out_ref[NBLK - 1 : NBLK, :] = jnp.sum(f0, axis=0, keepdims=True)
    out_ref[NBLK - 2 : NBLK - 1, :] = jnp.sum(f1, axis=0, keepdims=True)


def two(x):
    high = rounded(x)
    return high, x - high


def adj_left(v):
    left, _ = forms(v)
    row = lax.broadcasted_iota(jnp.int32, (8, BLOCK), 0)
    mass = v[6:7]
    radius = v[7:8]
    x = jnp.where(row < 4, mass, jnp.where(row < 8, mass * radius, 0.0))
    h, m = two(x)
    first = jnp.where(row % 4 < 2, h, m)
    h, m = two(jnp.where(row < 4, mass * radius * radius, 0.0))
    second = jnp.where(row % 4 < 2, h, m)
    zero = jnp.zeros((8, BLOCK), F32)
    return stacked(left[:5] + [first, second, zero])


def adj_right(v):
    _, right = forms(v)
    row = lax.broadcasted_iota(jnp.int32, (8, BLOCK), 0)
    radius = v[7:8]
    h, m = two(jnp.where(row < 4, radius * radius, 2.0 * radius))
    first = jnp.where(row % 2 == 0, h, m)
    second = jnp.where((row < 4) & (row % 2 == 0), 1.0, 0.0)
    zero = jnp.zeros((8, BLOCK), F32)
    arg = right[:5] + [zero, zero, zero]
    reach = [zero] * 5 + [first, second, zero]
    return jnp.concatenate([stacked(arg), stacked(reach)], axis=1)


def adj_kernel(o_ref, up_ref, down_ref, gain_ref, pairs_ref, list_ref, count_ref, out_ref, xt_ref, r_ref, found_ref):
    def build(j, carry):
        for half, ref in ((0, up_ref), (1, down_ref)):
            xt_ref[j + half * EDGE] = adj_left(ref[j]).T
            r_ref[j + half * EDGE] = adj_right(o_ref[j + half * (NBLK - EDGE)])
        return carry

    lax.fori_loop(0, EDGE, build, 0, unroll=8)
    count = count_ref[0, 0]
    found_ref[...] = jnp.zeros_like(found_ref)

    def main(u, carry):
        for x in range(ADJ_UNROLL):
            t = u * ADJ_UNROLL + x
            i = pairs_ref[0, t]
            j = jnp.clip(pairs_ref[1, t], 0, 2 * EDGE - 1)
            k = jnp.clip(jnp.where(i < EDGE, i, i - (NBLK - 2 * EDGE)), 0, 2 * EDGE - 1)
            d = jnp.dot(xt_ref[j], r_ref[k], preferred_element_type=F32)
            e = jnp.exp2(d[:, :BLOCK]) * d[:, BLOCK:]
            found_ref[pl.ds(t, 1), :] = jnp.sum(e, axis=0, keepdims=True)
        return carry

    lax.fori_loop(0, (count + ADJ_UNROLL - 1) // ADJ_UNROLL, main, 0)
    live = lax.broadcasted_iota(jnp.int32, (1, PADJ), 1) < count
    owner = onehot_rows(NBLK, jnp.where(live, list_ref[0:1, :], -1)).astype(BF)
    h, m = two(found_ref[...])
    h2, m2 = two(m)
    total = gain_ref[...]
    for part in (m2, h2, h):
        total = total + jnp.dot(owner, part.astype(BF), preferred_element_type=F32)
    out_ref[...] = total


def gather_kernel(gain_ref, slot_ref, attr_ref, out_ref):
    turned = gain_ref[...].T
    high, rest = two(turned)
    table = jnp.concatenate([high, rest], axis=1).astype(BF)
    number = lax.broadcasted_iota(jnp.int32, (NBLK, GCHUNK), 0).astype(F32).astype(BF)

    def step(s, carry):
        low = pl.multiple_of(s * GCHUNK, GCHUNK)
        slot = slot_ref[:, pl.ds(low, GCHUNK)]
        block = number == (slot >> 7).astype(F32).astype(BF)
        block = jnp.where(block, jnp.ones((), BF), jnp.zeros((), BF))
        z = jnp.dot(table, jnp.concatenate([block, block], axis=0), preferred_element_type=F32)
        lane = lax.broadcasted_iota(jnp.int32, (BLOCK, GCHUNK), 0) == (slot & 127)
        gain = jnp.sum(jnp.where(lane, z, 0.0), axis=0, keepdims=True)
        out_ref[:, pl.ds(low, GCHUNK)] = attr_ref[6:7, pl.ds(low, GCHUNK)] + RATE * gain
        return carry

    lax.fori_loop(0, FLOC_DEV // GCHUNK, step, 0, unroll=2)


VMEM = pl.BlockSpec(memory_space=pltpu.VMEM)
SMEM = pl.BlockSpec(memory_space=pltpu.SMEM)
HBM = pl.BlockSpec(memory_space=pltpu.HBM)


def call(kernel, name, out, ins, scratch, cost, *args):
    return pl.pallas_call(
        kernel,
        out_shape=out,
        in_specs=ins,
        out_specs=jax.tree.map(lambda _: VMEM, out),
        scratch_shapes=scratch,
        compiler_params=pltpu.CompilerParams(vmem_limit_bytes=(60 if name == "scatter" else 52) * MIB),
        cost_estimate=pl.CostEstimate(flops=cost, bytes_accessed=2 * MIB, transcendentals=0),
        name=name,
    )(*args)


def shape(*dims):
    return jax.ShapeDtypeStruct(dims, F32)


def body(floc_attr, floc_slot, same_pairs, same_count, adj_pairs, neighbour_pair_count):
    tiles = lax.axis_size("tile")
    cap_blocks = NBLK // tiles
    segs = lax.axis_size("seg")
    slot_row = floc_slot.reshape(1, FLOC_DEV)
    send, mult, adj_list = call(
        scatter_kernel,
        "scatter",
        (shape(NBLK, ATTR, BLOCK), shape(8, NBLK), jax.ShapeDtypeStruct((2, PADJ), jnp.int32)),
        [HBM, HBM, HBM, HBM, SMEM],
        [
            pltpu.VMEM((ATTR, FLOC_DEV), F32),
            pltpu.VMEM((1, FLOC_DEV), jnp.int32),
            pltpu.VMEM((2, PSAME), jnp.int32),
            pltpu.SemaphoreType.DMA((4,)),
            pltpu.VMEM((ATTR * BLOCK, 2 * CHUNK), BF),
            pltpu.VMEM((ATTR * BLOCK, 2 * CHUNK), BF),
            pltpu.VMEM((NBLK, 2 * CHUNK), BF),
            pltpu.VMEM((NBLK, 2 * CHUNK), BF),
            pltpu.VMEM((ATTR * BLOCK, NBLK), F32),
        ],
        2 * 2 * ATTR * BLOCK * NBLK * FLOC_DEV,
        floc_attr,
        slot_row,
        same_pairs.reshape(2, PSAME),
        adj_pairs.reshape(2, PADJ),
        same_count,
    )
    send = send.reshape(tiles, cap_blocks, ATTR, BLOCK)
    owned = lax.all_to_all(send, "tile", split_axis=0, concat_axis=0, tiled=True)
    owned = owned.reshape(NBLK, ATTR, BLOCK)
    up = lax.ppermute(owned[NBLK - EDGE :], "seg", [(i, i + 1) for i in range(segs - 1)])
    down = lax.ppermute(owned[:EDGE], "seg", [(i + 1, i) for i in range(segs - 1)])
    gain = call(
        same_kernel,
        "same_pairs",
        shape(NBLK, BLOCK),
        [VMEM, SMEM],
        [
            pltpu.VMEM((GROUP, BLOCK, KF), BF),
            pltpu.VMEM((GROUP, BLOCK, KF), BF),
            pltpu.VMEM((GROUP + 2, KF, BLOCK), BF),
            pltpu.VMEM((GROUP + 2, KF, BLOCK), BF),
        ],
        40_000_000_000,
        owned,
        mult,
    )
    gain = call(
        adj_kernel,
        "adjacent_pairs",
        shape(NBLK, BLOCK),
        [VMEM, VMEM, VMEM, VMEM, SMEM, VMEM, SMEM],
        [
            pltpu.VMEM((2 * EDGE, BLOCK, KADJ), BF),
            pltpu.VMEM((2 * EDGE, KADJ, 2 * BLOCK), BF),
            pltpu.VMEM((PADJ, BLOCK), F32),
        ],
        10_000_000_000,
        owned,
        up,
        down,
        gain,
        adj_list,
        adj_list,
        neighbour_pair_count,
    )
    gain = gain.reshape(tiles, cap_blocks, BLOCK)
    returned = lax.all_to_all(gain, "tile", split_axis=0, concat_axis=0, tiled=True)
    out = call(
        gather_kernel,
        "final_gather",
        shape(1, FLOC_DEV),
        [VMEM, VMEM, VMEM],
        [],
        10_000_000_000,
        returned.reshape(NBLK, BLOCK),
        slot_row,
        floc_attr,
    )
    return out.reshape(FLOC_DEV)


def solution(mesh):
    placed = (
        P(None, ("seg", "tile")),
        P(("seg", "tile")),
        P("seg", "tile", None, None),
        P("seg", "tile"),
        P("seg", "tile", None, None),
        P("seg", "tile"),
    )
    return jax.shard_map(
        body, mesh=mesh, in_specs=placed, out_specs=P(("seg", "tile")), check_vma=False
    )
```

```python
import functools

import jax
import jax.numpy as jnp
import numpy as np
from jax import lax
from jax.experimental import pallas as pl
from jax.experimental.pallas import tpu as pltpu
from jax.sharding import PartitionSpec as P

ATTR = 8
BLOCK = 128
FLOC_DEV = 16384
NBLK = 256
EDGE = 32
RATE = 0.05
PSAME = 1024
PADJ = 128
SCALE = float(np.sqrt(np.log2(np.e)))
CHUNK = 2048
GCHUNK = 1024
KF = 48
KADJ = 64
GROUP = 16
ADJ_UNROLL = 64
QROWS = 32
MIB = 2**20
BF = jnp.bfloat16
F32 = jnp.float32


def rounded(x):
    return x.astype(BF).astype(F32)


def onehot_rows(rows, index):
    shape = (rows, index.shape[1])
    return jnp.where(lax.broadcasted_iota(jnp.int32, shape, 0) == index, 1.0, 0.0)


def fetch(sources, targets, sems):
    copies = [
        pltpu.make_async_copy(source, target, sems.at[n])
        for n, (source, target) in enumerate(zip(sources, targets))
    ]
    for copy in copies:
        copy.start()
    return copies


def scatter_kernel(
    attr_hbm, slot_hbm, pairs_hbm, adj_hbm, count_ref, out_ref, mult_ref, adj_ref,
    attr_ref, slot_ref, pairs_ref, sems, y0, y1, b0, b1, acc_ref,
):
    copies = fetch(
        (attr_hbm, slot_hbm, pairs_hbm, adj_hbm), (attr_ref, slot_ref, pairs_ref, adj_ref), sems
    )
    acc_ref[...] = jnp.zeros_like(acc_ref)
    copies[2].wait()
    first = pairs_ref[0:1, :]
    offset = pairs_ref[1:2, :] - first + 2
    live = lax.broadcasted_iota(jnp.int32, (1, PSAME), 1) < count_ref[0, 0]
    offset = jnp.where(live, offset, -1)
    mult_ref[...] = lax.dot_general(
        onehot_rows(8, offset).astype(BF),
        onehot_rows(NBLK, first).astype(BF),
        (((1,), (1,)), ((), ())),
        preferred_element_type=F32,
    )
    number = lax.broadcasted_iota(jnp.int32, (NBLK, CHUNK), 0).astype(F32).astype(BF)
    row = lax.broadcasted_iota(jnp.int32, (ATTR, CHUNK), 0)
    zero = jnp.zeros((), BF)
    chunks = FLOC_DEV // CHUNK

    def spread(s, y_ref, b_ref):
        low = pl.multiple_of(s * CHUNK, CHUNK)
        slot = slot_ref[:, pl.ds(low, CHUNK)]
        block = jnp.where(number == (slot >> 7).astype(F32).astype(BF), jnp.ones((), BF), zero)
        b_ref[:, :CHUNK] = block
        b_ref[:, CHUNK:] = block
        lane = number[:BLOCK] == (slot & 127).astype(F32).astype(BF)
        value = attr_ref[:, pl.ds(low, CHUNK)]
        value = jnp.where(row < 6, value * SCALE, value)
        high = value.astype(BF)
        rest = (value - high.astype(F32)).astype(BF)
        for a in range(ATTR):
            at = slice(a * BLOCK, (a + 1) * BLOCK)
            y_ref[at, :CHUNK] = jnp.where(lane, high[a : a + 1], zero)
            y_ref[at, CHUNK:] = jnp.where(lane, rest[a : a + 1], zero)

    def place(y_ref, b_ref):
        acc_ref[...] += lax.dot_general(
            y_ref[...], b_ref[...], (((1,), (1,)), ((), ())), preferred_element_type=F32
        )

    def step(u, carry):
        spread(2 * u + 1, y1, b1)
        place(y0, b0)
        spread(jnp.minimum(2 * u + 2, chunks - 1), y0, b0)
        place(y1, b1)
        return carry

    for n in (0, 1, 3):
        copies[n].wait()
    spread(0, y0, b0)
    lax.fori_loop(0, chunks // 2, step, 0)
    for a in range(ATTR):
        out_ref[:, a, :] = acc_ref[a * BLOCK : (a + 1) * BLOCK, :].T


def forms(v):
    row = lax.broadcasted_iota(jnp.int32, (8, BLOCK), 0)
    six = row < 6
    lo3 = row < 3
    high = rounded(v)
    rest = v - high
    norm = -0.5 * jnp.sum(jnp.where(six, v * v, 0.0), axis=0, keepdims=True)
    n0 = rounded(norm)
    n1 = rounded(norm - n0)
    n2 = norm - n0 - n1
    k = jnp.where(lo3, row, row - 3)
    parts = jnp.where(k == 0, n0, jnp.where(k == 1, n1, n2))
    one = jnp.where(six, 1.0, 0.0)
    h6 = jnp.where(six, high, 0.0)
    m6 = jnp.where(six, rest, 0.0)
    zero = jnp.zeros((8, BLOCK), F32)
    left = [high, rest, high, rest, jnp.where(lo3, parts, one), zero]
    right = [h6, m6, m6, h6, jnp.where(lo3, one, jnp.where(six, parts, 0.0)), zero]
    return left, right


def stacked(rows):
    return jnp.concatenate(rows, axis=0).astype(BF)


def spread_form():
    row = lax.broadcasted_iota(jnp.int32, (KF, 2 * BLOCK), 0)
    lane = lax.broadcasted_iota(jnp.int32, (KF, 2 * BLOCK), 1)
    want = jnp.where(lane < BLOCK, 6, 7)
    return jnp.where((row == want) | (row == want + 8), 1.0, 0.0).astype(BF)


def same_kernel(o_ref, mult_ref, list_ref, out_ref, adj_ref, xt0, xt1, r0, r1):
    adj_ref[...] = list_ref[...]
    spread = spread_form()
    shape8 = (8, BLOCK)
    diff = lax.broadcasted_iota(jnp.int32, shape8, 1) - lax.broadcasted_iota(jnp.int32, shape8, 0)

    def build(j, x, xt_ref, r_ref):
        left, right = forms(o_ref[j])
        r_ref[x + 2] = stacked(right)
        xt_ref[x] = stacked(left).T

    def main(j, x, xt_ref, r_ref, carry):
        f1, f2 = carry
        j1 = jnp.maximum(j - 1, 0)
        j2 = jnp.maximum(j - 2, 0)
        own = [o_ref[j], o_ref[j1], o_ref[j2]]
        radius = [jnp.broadcast_to(o[7:8], shape8) for o in own]
        mass1 = own[1][6:7] * mult_ref[1, j]
        mass2 = own[2][6:7] * mult_ref[0, j]
        rhs = jnp.concatenate([r_ref[x + 2], r_ref[x + 1], r_ref[x], spread], axis=1)
        acc = [jnp.zeros(shape8, F32) for _ in range(3)]
        rev = []
        for q in range(0, BLOCK, QROWS):
            d = jnp.dot(xt_ref[x, q : q + QROWS, :], rhs, preferred_element_type=F32)
            for s in range(0, QROWS, 8):
                z = d[s : s + 8]
                mass = z[:, 3 * BLOCK : 4 * BLOCK]
                reach = z[:, 4 * BLOCK : 5 * BLOCK]
                w = []
                for a in range(3):
                    t = reach + radius[a]
                    e = jnp.exp2(z[:, a * BLOCK : (a + 1) * BLOCK]) * (t * t)
                    if a == 0:
                        e = jnp.where(diff == q + s, 0.0, e)
                    w.append(e)
                    acc[a] = acc[a] + e * mass
                rev.append(w[1] * mass1 + w[2] * mass2)
        back = jnp.sum(jnp.concatenate(rev, axis=0).T.reshape(BLOCK // 8, 8, BLOCK), axis=0)
        f0 = acc[0] * mult_ref[2, j] + back
        f1 = f1 + acc[1] * mult_ref[3, j1]
        f2 = f2 + acc[2] * mult_ref[4, j2]
        out_ref[pl.ds(j2, 1), :] = jnp.sum(f2, axis=0, keepdims=True)
        return f0, f1

    r0[0] = jnp.zeros((KF, BLOCK), BF)
    r0[1] = jnp.zeros((KF, BLOCK), BF)
    for x in range(GROUP):
        build(x, x, xt0, r0)

    def groups(u, carry):
        for half, (xa, ra, xb, rb) in enumerate(((xt0, r0, xt1, r1), (xt1, r1, xt0, r0))):
            base = (2 * u + half) * GROUP
            later = jnp.minimum(base + GROUP, NBLK - GROUP)
            rb[0] = ra[GROUP]
            rb[1] = ra[GROUP + 1]
            for x in range(GROUP):
                build(later + x, x, xb, rb)
                carry = main(base + x, x, xa, ra, carry)
        return carry

    zero = jnp.zeros(shape8, F32)
    f0, f1 = lax.fori_loop(0, NBLK // (2 * GROUP), groups, (zero, zero))
    out_ref[NBLK - 1 : NBLK, :] = jnp.sum(f0, axis=0, keepdims=True)
    out_ref[NBLK - 2 : NBLK - 1, :] = jnp.sum(f1, axis=0, keepdims=True)


def two(x):
    high = rounded(x)
    return high, x - high


def adj_left(v):
    left, _ = forms(v)
    row = lax.broadcasted_iota(jnp.int32, (8, BLOCK), 0)
    mass = v[6:7]
    radius = v[7:8]
    x = jnp.where(row < 4, mass, jnp.where(row < 8, mass * radius, 0.0))
    h, m = two(x)
    first = jnp.where(row % 4 < 2, h, m)
    h, m = two(jnp.where(row < 4, mass * radius * radius, 0.0))
    second = jnp.where(row % 4 < 2, h, m)
    zero = jnp.zeros((8, BLOCK), F32)
    return stacked(left[:5] + [first, second, zero])


def adj_right(v):
    _, right = forms(v)
    row = lax.broadcasted_iota(jnp.int32, (8, BLOCK), 0)
    radius = v[7:8]
    h, m = two(jnp.where(row < 4, radius * radius, 2.0 * radius))
    first = jnp.where(row % 2 == 0, h, m)
    second = jnp.where((row < 4) & (row % 2 == 0), 1.0, 0.0)
    zero = jnp.zeros((8, BLOCK), F32)
    arg = right[:5] + [zero, zero, zero]
    reach = [zero] * 5 + [first, second, zero]
    return jnp.concatenate([stacked(arg), stacked(reach)], axis=1)


def adj_kernel(o_ref, up_ref, down_ref, gain_ref, pairs_ref, list_ref, count_ref, out_ref, xt_ref, r_ref, found_ref):
    def build(j, carry):
        for half, ref in ((0, up_ref), (1, down_ref)):
            xt_ref[j + half * EDGE] = adj_left(ref[j]).T
            r_ref[j + half * EDGE] = adj_right(o_ref[j + half * (NBLK - EDGE)])
        return carry

    lax.fori_loop(0, EDGE, build, 0, unroll=16)
    count = count_ref[0, 0]
    found_ref[...] = jnp.zeros_like(found_ref)

    def main(u, carry):
        for x in range(ADJ_UNROLL):
            t = u * ADJ_UNROLL + x
            i = pairs_ref[0, t]
            j = jnp.clip(pairs_ref[1, t], 0, 2 * EDGE - 1)
            k = jnp.clip(jnp.where(i < EDGE, i, i - (NBLK - 2 * EDGE)), 0, 2 * EDGE - 1)
            d = jnp.dot(xt_ref[j], r_ref[k], preferred_element_type=F32)
            e = jnp.exp2(d[:, :BLOCK]) * d[:, BLOCK:]
            found_ref[pl.ds(t, 1), :] = jnp.sum(e, axis=0, keepdims=True)
        return carry

    lax.fori_loop(0, (count + ADJ_UNROLL - 1) // ADJ_UNROLL, main, 0)
    live = lax.broadcasted_iota(jnp.int32, (1, PADJ), 1) < count
    owner = onehot_rows(NBLK, jnp.where(live, list_ref[0:1, :], -1)).astype(BF)
    h, m = two(found_ref[...])
    h2, m2 = two(m)
    total = gain_ref[...]
    for part in (m2, h2, h):
        total = total + jnp.dot(owner, part.astype(BF), preferred_element_type=F32)
    out_ref[...] = total


def gather_kernel(gain_ref, slot_ref, attr_ref, out_ref):
    turned = gain_ref[...].T
    high, rest = two(turned)
    table = jnp.concatenate([high, rest], axis=1).astype(BF)
    number = lax.broadcasted_iota(jnp.int32, (NBLK, GCHUNK), 0).astype(F32).astype(BF)

    def step(s, carry):
        low = pl.multiple_of(s * GCHUNK, GCHUNK)
        slot = slot_ref[:, pl.ds(low, GCHUNK)]
        block = number == (slot >> 7).astype(F32).astype(BF)
        block = jnp.where(block, jnp.ones((), BF), jnp.zeros((), BF))
        z = jnp.dot(table, jnp.concatenate([block, block], axis=0), preferred_element_type=F32)
        lane = lax.broadcasted_iota(jnp.int32, (BLOCK, GCHUNK), 0) == (slot & 127)
        gain = jnp.sum(jnp.where(lane, z, 0.0), axis=0, keepdims=True)
        out_ref[:, pl.ds(low, GCHUNK)] = attr_ref[6:7, pl.ds(low, GCHUNK)] + RATE * gain
        return carry

    lax.fori_loop(0, FLOC_DEV // GCHUNK, step, 0, unroll=16)


VMEM = pl.BlockSpec(memory_space=pltpu.VMEM)
SMEM = pl.BlockSpec(memory_space=pltpu.SMEM)
HBM = pl.BlockSpec(memory_space=pltpu.HBM)


def call(kernel, name, out, ins, scratch, cost, *args):
    return pl.pallas_call(
        kernel,
        out_shape=out,
        in_specs=ins,
        out_specs=jax.tree.map(lambda _: VMEM, out),
        scratch_shapes=scratch,
        compiler_params=pltpu.CompilerParams(vmem_limit_bytes=(60 if name == "scatter" else 52) * MIB),
        cost_estimate=pl.CostEstimate(flops=cost, bytes_accessed=2 * MIB, transcendentals=0),
        name=name,
    )(*args)


def shape(*dims):
    return jax.ShapeDtypeStruct(dims, F32)


def body(floc_attr, floc_slot, same_pairs, same_count, adj_pairs, neighbour_pair_count):
    tiles = lax.axis_size("tile")
    cap_blocks = NBLK // tiles
    segs = lax.axis_size("seg")
    slot_row = floc_slot.reshape(1, FLOC_DEV)
    send, mult, adj_list = call(
        scatter_kernel,
        "scatter",
        (shape(NBLK, ATTR, BLOCK), shape(8, NBLK), jax.ShapeDtypeStruct((2, PADJ), jnp.int32)),
        [HBM, HBM, HBM, HBM, SMEM],
        [
            pltpu.VMEM((ATTR, FLOC_DEV), F32),
            pltpu.VMEM((1, FLOC_DEV), jnp.int32),
            pltpu.VMEM((2, PSAME), jnp.int32),
            pltpu.SemaphoreType.DMA((4,)),
            pltpu.VMEM((ATTR * BLOCK, 2 * CHUNK), BF),
            pltpu.VMEM((ATTR * BLOCK, 2 * CHUNK), BF),
            pltpu.VMEM((NBLK, 2 * CHUNK), BF),
            pltpu.VMEM((NBLK, 2 * CHUNK), BF),
            pltpu.VMEM((ATTR * BLOCK, NBLK), F32),
        ],
        2 * 2 * ATTR * BLOCK * NBLK * FLOC_DEV,
        floc_attr,
        slot_row,
        same_pairs.reshape(2, PSAME),
        adj_pairs.reshape(2, PADJ),
        same_count,
    )
    send = send.reshape(tiles, cap_blocks, ATTR, BLOCK)
    owned = lax.all_to_all(send, "tile", split_axis=0, concat_axis=0, tiled=True)
    owned = owned.reshape(NBLK, ATTR, BLOCK)
    up = lax.ppermute(owned[NBLK - EDGE :], "seg", [(i, i + 1) for i in range(segs - 1)])
    down = lax.ppermute(owned[:EDGE], "seg", [(i + 1, i) for i in range(segs - 1)])
    gain, adj_list = call(
        same_kernel,
        "same_pairs",
        (shape(NBLK, BLOCK), jax.ShapeDtypeStruct((2, PADJ), jnp.int32)),
        [VMEM, SMEM, VMEM],
        [
            pltpu.VMEM((GROUP, BLOCK, KF), BF),
            pltpu.VMEM((GROUP, BLOCK, KF), BF),
            pltpu.VMEM((GROUP + 2, KF, BLOCK), BF),
            pltpu.VMEM((GROUP + 2, KF, BLOCK), BF),
        ],
        40_000_000_000,
        owned,
        mult,
        adj_list,
    )
    gain = call(
        adj_kernel,
        "adjacent_pairs",
        shape(NBLK, BLOCK),
        [VMEM, VMEM, VMEM, VMEM, SMEM, VMEM, SMEM],
        [
            pltpu.VMEM((2 * EDGE, BLOCK, KADJ), BF),
            pltpu.VMEM((2 * EDGE, KADJ, 2 * BLOCK), BF),
            pltpu.VMEM((PADJ, BLOCK), F32),
        ],
        10_000_000_000,
        owned,
        up,
        down,
        gain,
        adj_list,
        adj_list,
        neighbour_pair_count,
    )
    gain = gain.reshape(tiles, cap_blocks, BLOCK)
    returned = lax.all_to_all(gain, "tile", split_axis=0, concat_axis=0, tiled=True)
    out = call(
        gather_kernel,
        "final_gather",
        shape(1, FLOC_DEV),
        [VMEM, VMEM, VMEM],
        [],
        10_000_000_000,
        returned.reshape(NBLK, BLOCK),
        slot_row,
        floc_attr,
    )
    return out.reshape(FLOC_DEV)


def solution(mesh):
    placed = (
        P(None, ("seg", "tile")),
        P(("seg", "tile")),
        P("seg", "tile", None, None),
        P("seg", "tile"),
        P("seg", "tile", None, None),
        P("seg", "tile"),
    )
    return jax.shard_map(
        body, mesh=mesh, in_specs=placed, out_specs=P(("seg", "tile")), check_vma=False
    )
```

```python
import functools

import jax
import jax.numpy as jnp
import numpy as np
from jax import lax
from jax.experimental import pallas as pl
from jax.experimental.pallas import tpu as pltpu
from jax.sharding import PartitionSpec as P

ATTR = 8
BLOCK = 128
FLOC_DEV = 16384
NBLK = 256
EDGE = 32
RATE = 0.05
PSAME = 1024
PADJ = 128
SCALE = float(np.sqrt(np.log2(np.e)))
CHUNK = 2048
GCHUNK = 1024
KF = 48
KADJ = 64
GROUP = 16
ADJ_UNROLL = 64
QROWS = 32
MIB = 2**20
BF = jnp.bfloat16
F32 = jnp.float32


def rounded(x):
    return x.astype(BF).astype(F32)


def onehot_rows(rows, index):
    shape = (rows, index.shape[1])
    return jnp.where(lax.broadcasted_iota(jnp.int32, shape, 0) == index, 1.0, 0.0)


def fetch(sources, targets, sems):
    copies = [
        pltpu.make_async_copy(source, target, sems.at[n])
        for n, (source, target) in enumerate(zip(sources, targets))
    ]
    for copy in copies:
        copy.start()
    return copies


def scatter_kernel(
    attr_hbm, slot_hbm, pairs_hbm, count_ref, out_ref, mult_ref,
    attr_ref, slot_ref, pairs_ref, sems, y0, y1, b0, b1, acc_ref,
):
    copies = fetch((attr_hbm, slot_hbm, pairs_hbm), (attr_ref, slot_ref, pairs_ref), sems)
    acc_ref[...] = jnp.zeros_like(acc_ref)
    copies[2].wait()
    first = pairs_ref[0:1, :]
    offset = pairs_ref[1:2, :] - first + 2
    live = lax.broadcasted_iota(jnp.int32, (1, PSAME), 1) < count_ref[0, 0]
    offset = jnp.where(live, offset, -1)
    mult_ref[...] = lax.dot_general(
        onehot_rows(8, offset).astype(BF),
        onehot_rows(NBLK, first).astype(BF),
        (((1,), (1,)), ((), ())),
        preferred_element_type=F32,
    )
    number = lax.broadcasted_iota(jnp.int32, (NBLK, CHUNK), 0).astype(F32).astype(BF)
    row = lax.broadcasted_iota(jnp.int32, (ATTR, CHUNK), 0)
    zero = jnp.zeros((), BF)
    chunks = FLOC_DEV // CHUNK

    def spread(s, y_ref, b_ref):
        low = pl.multiple_of(s * CHUNK, CHUNK)
        slot = slot_ref[:, pl.ds(low, CHUNK)]
        block = jnp.where(number == (slot >> 7).astype(F32).astype(BF), jnp.ones((), BF), zero)
        b_ref[:, :CHUNK] = block
        b_ref[:, CHUNK:] = block
        lane = number[:BLOCK] == (slot & 127).astype(F32).astype(BF)
        value = attr_ref[:, pl.ds(low, CHUNK)]
        value = jnp.where(row < 6, value * SCALE, value)
        high = value.astype(BF)
        rest = (value - high.astype(F32)).astype(BF)
        for a in range(ATTR):
            at = slice(a * BLOCK, (a + 1) * BLOCK)
            y_ref[at, :CHUNK] = jnp.where(lane, high[a : a + 1], zero)
            y_ref[at, CHUNK:] = jnp.where(lane, rest[a : a + 1], zero)

    def place(y_ref, b_ref):
        acc_ref[...] += lax.dot_general(
            y_ref[...], b_ref[...], (((1,), (1,)), ((), ())), preferred_element_type=F32
        )

    def step(u, carry):
        spread(2 * u + 1, y1, b1)
        place(y0, b0)
        spread(jnp.minimum(2 * u + 2, chunks - 1), y0, b0)
        place(y1, b1)
        return carry

    for n in (0, 1):
        copies[n].wait()
    spread(0, y0, b0)
    lax.fori_loop(0, chunks // 2, step, 0)
    for a in range(ATTR):
        out_ref[:, a, :] = acc_ref[a * BLOCK : (a + 1) * BLOCK, :].T


def forms(v):
    row = lax.broadcasted_iota(jnp.int32, (8, BLOCK), 0)
    six = row < 6
    lo3 = row < 3
    high = rounded(v)
    rest = v - high
    norm = -0.5 * jnp.sum(jnp.where(six, v * v, 0.0), axis=0, keepdims=True)
    n0 = rounded(norm)
    n1 = rounded(norm - n0)
    n2 = norm - n0 - n1
    k = jnp.where(lo3, row, row - 3)
    parts = jnp.where(k == 0, n0, jnp.where(k == 1, n1, n2))
    one = jnp.where(six, 1.0, 0.0)
    h6 = jnp.where(six, high, 0.0)
    m6 = jnp.where(six, rest, 0.0)
    zero = jnp.zeros((8, BLOCK), F32)
    left = [high, rest, high, rest, jnp.where(lo3, parts, one), zero]
    right = [h6, m6, m6, h6, jnp.where(lo3, one, jnp.where(six, parts, 0.0)), zero]
    return left, right


def stacked(rows):
    return jnp.concatenate(rows, axis=0).astype(BF)


def spread_form():
    row = lax.broadcasted_iota(jnp.int32, (KF, 2 * BLOCK), 0)
    lane = lax.broadcasted_iota(jnp.int32, (KF, 2 * BLOCK), 1)
    want = jnp.where(lane < BLOCK, 6, 7)
    return jnp.where((row == want) | (row == want + 8), 1.0, 0.0).astype(BF)


def same_kernel(o_ref, mult_ref, list_ref, out_ref, adj_ref, xt0, xt1, r0, r1):
    adj_ref[...] = list_ref[...]
    spread = spread_form()
    shape8 = (8, BLOCK)
    diff = lax.broadcasted_iota(jnp.int32, shape8, 1) - lax.broadcasted_iota(jnp.int32, shape8, 0)

    def build(j, x, xt_ref, r_ref):
        left, right = forms(o_ref[j])
        r_ref[x + 2] = stacked(right)
        xt_ref[x] = stacked(left).T

    def main(j, x, xt_ref, r_ref, carry):
        f1, f2 = carry
        j1 = jnp.maximum(j - 1, 0)
        j2 = jnp.maximum(j - 2, 0)
        own = [o_ref[j], o_ref[j1], o_ref[j2]]
        radius = [jnp.broadcast_to(o[7:8], shape8) for o in own]
        mass1 = own[1][6:7] * mult_ref[1, j]
        mass2 = own[2][6:7] * mult_ref[0, j]
        rhs = jnp.concatenate([r_ref[x + 2], r_ref[x + 1], r_ref[x], spread], axis=1)
        acc = [jnp.zeros(shape8, F32) for _ in range(3)]
        rev = []
        for q in range(0, BLOCK, QROWS):
            d = jnp.dot(xt_ref[x, q : q + QROWS, :], rhs, preferred_element_type=F32)
            for s in range(0, QROWS, 8):
                z = d[s : s + 8]
                mass = z[:, 3 * BLOCK : 4 * BLOCK]
                reach = z[:, 4 * BLOCK : 5 * BLOCK]
                w = []
                for a in range(3):
                    t = reach + radius[a]
                    e = jnp.exp2(z[:, a * BLOCK : (a + 1) * BLOCK]) * (t * t)
                    if a == 0:
                        e = jnp.where(diff == q + s, 0.0, e)
                    w.append(e)
                    acc[a] = acc[a] + e * mass
                rev.append(w[1] * mass1 + w[2] * mass2)
        back = jnp.sum(jnp.concatenate(rev, axis=0).T.reshape(BLOCK // 8, 8, BLOCK), axis=0)
        f0 = acc[0] * mult_ref[2, j] + back
        f1 = f1 + acc[1] * mult_ref[3, j1]
        f2 = f2 + acc[2] * mult_ref[4, j2]
        out_ref[pl.ds(j2, 1), :] = jnp.sum(f2, axis=0, keepdims=True)
        return f0, f1

    r0[0] = jnp.zeros((KF, BLOCK), BF)
    r0[1] = jnp.zeros((KF, BLOCK), BF)
    for x in range(GROUP):
        build(x, x, xt0, r0)

    def groups(u, carry):
        for half, (xa, ra, xb, rb) in enumerate(((xt0, r0, xt1, r1), (xt1, r1, xt0, r0))):
            base = (2 * u + half) * GROUP
            later = jnp.minimum(base + GROUP, NBLK - GROUP)
            rb[0] = ra[GROUP]
            rb[1] = ra[GROUP + 1]
            for x in range(GROUP):
                build(later + x, x, xb, rb)
                carry = main(base + x, x, xa, ra, carry)
        return carry

    zero = jnp.zeros(shape8, F32)
    f0, f1 = lax.fori_loop(0, NBLK // (2 * GROUP), groups, (zero, zero))
    out_ref[NBLK - 1 : NBLK, :] = jnp.sum(f0, axis=0, keepdims=True)
    out_ref[NBLK - 2 : NBLK - 1, :] = jnp.sum(f1, axis=0, keepdims=True)


def two(x):
    high = rounded(x)
    return high, x - high


def adj_left(v):
    left, _ = forms(v)
    row = lax.broadcasted_iota(jnp.int32, (8, BLOCK), 0)
    mass = v[6:7]
    radius = v[7:8]
    x = jnp.where(row < 4, mass, jnp.where(row < 8, mass * radius, 0.0))
    h, m = two(x)
    first = jnp.where(row % 4 < 2, h, m)
    h, m = two(jnp.where(row < 4, mass * radius * radius, 0.0))
    second = jnp.where(row % 4 < 2, h, m)
    zero = jnp.zeros((8, BLOCK), F32)
    return stacked(left[:5] + [first, second, zero])


def adj_right(v):
    _, right = forms(v)
    row = lax.broadcasted_iota(jnp.int32, (8, BLOCK), 0)
    radius = v[7:8]
    h, m = two(jnp.where(row < 4, radius * radius, 2.0 * radius))
    first = jnp.where(row % 2 == 0, h, m)
    second = jnp.where((row < 4) & (row % 2 == 0), 1.0, 0.0)
    zero = jnp.zeros((8, BLOCK), F32)
    arg = right[:5] + [zero, zero, zero]
    reach = [zero] * 5 + [first, second, zero]
    return jnp.concatenate([stacked(arg), stacked(reach)], axis=1)


def adj_kernel(o_ref, up_ref, down_ref, gain_ref, pairs_ref, list_ref, count_ref, out_ref, xt_ref, r_ref, found_ref):
    def build(j, carry):
        for half, ref in ((0, up_ref), (1, down_ref)):
            xt_ref[j + half * EDGE] = adj_left(ref[j]).T
            r_ref[j + half * EDGE] = adj_right(o_ref[j + half * (NBLK - EDGE)])
        return carry

    lax.fori_loop(0, EDGE, build, 0, unroll=16)
    count = count_ref[0, 0]
    found_ref[...] = jnp.zeros_like(found_ref)

    def main(u, carry):
        for x in range(ADJ_UNROLL):
            t = u * ADJ_UNROLL + x
            i = pairs_ref[0, t]
            j = jnp.clip(pairs_ref[1, t], 0, 2 * EDGE - 1)
            k = jnp.clip(jnp.where(i < EDGE, i, i - (NBLK - 2 * EDGE)), 0, 2 * EDGE - 1)
            d = jnp.dot(xt_ref[j], r_ref[k], preferred_element_type=F32)
            e = jnp.exp2(d[:, :BLOCK]) * d[:, BLOCK:]
            found_ref[pl.ds(t, 1), :] = jnp.sum(e, axis=0, keepdims=True)
        return carry

    lax.fori_loop(0, (count + ADJ_UNROLL - 1) // ADJ_UNROLL, main, 0)
    live = lax.broadcasted_iota(jnp.int32, (1, PADJ), 1) < count
    owner = onehot_rows(NBLK, jnp.where(live, list_ref[0:1, :], -1)).astype(BF)
    h, m = two(found_ref[...])
    h2, m2 = two(m)
    total = gain_ref[...]
    for part in (m2, h2, h):
        total = total + jnp.dot(owner, part.astype(BF), preferred_element_type=F32)
    out_ref[...] = total


def gather_kernel(gain_ref, slot_ref, attr_ref, out_ref):
    turned = gain_ref[...].T
    high, rest = two(turned)
    table = jnp.concatenate([high, rest], axis=1).astype(BF)
    number = lax.broadcasted_iota(jnp.int32, (NBLK, GCHUNK), 0).astype(F32).astype(BF)

    def step(s, carry):
        low = pl.multiple_of(s * GCHUNK, GCHUNK)
        slot = slot_ref[:, pl.ds(low, GCHUNK)]
        block = number == (slot >> 7).astype(F32).astype(BF)
        block = jnp.where(block, jnp.ones((), BF), jnp.zeros((), BF))
        z = jnp.dot(table, jnp.concatenate([block, block], axis=0), preferred_element_type=F32)
        lane = lax.broadcasted_iota(jnp.int32, (BLOCK, GCHUNK), 0) == (slot & 127)
        gain = jnp.sum(jnp.where(lane, z, 0.0), axis=0, keepdims=True)
        out_ref[:, pl.ds(low, GCHUNK)] = attr_ref[6:7, pl.ds(low, GCHUNK)] + RATE * gain
        return carry

    lax.fori_loop(0, FLOC_DEV // GCHUNK, step, 0, unroll=16)


VMEM = pl.BlockSpec(memory_space=pltpu.VMEM)
SMEM = pl.BlockSpec(memory_space=pltpu.SMEM)
HBM = pl.BlockSpec(memory_space=pltpu.HBM)


def call(kernel, name, out, ins, scratch, cost, *args):
    return pl.pallas_call(
        kernel,
        out_shape=out,
        in_specs=ins,
        out_specs=jax.tree.map(lambda _: VMEM, out),
        scratch_shapes=scratch,
        compiler_params=pltpu.CompilerParams(vmem_limit_bytes=(60 if name == "scatter" else 52) * MIB),
        cost_estimate=pl.CostEstimate(flops=cost, bytes_accessed=2 * MIB, transcendentals=0),
        name=name,
    )(*args)


def shape(*dims):
    return jax.ShapeDtypeStruct(dims, F32)


def body(floc_attr, floc_slot, same_pairs, same_count, adj_pairs, neighbour_pair_count):
    tiles = lax.axis_size("tile")
    cap_blocks = NBLK // tiles
    segs = lax.axis_size("seg")
    slot_row = floc_slot.reshape(1, FLOC_DEV)
    send, mult = call(
        scatter_kernel,
        "scatter",
        (shape(NBLK, ATTR, BLOCK), shape(8, NBLK)),
        [HBM, HBM, HBM, SMEM],
        [
            pltpu.VMEM((ATTR, FLOC_DEV), F32),
            pltpu.VMEM((1, FLOC_DEV), jnp.int32),
            pltpu.VMEM((2, PSAME), jnp.int32),
            pltpu.SemaphoreType.DMA((3,)),
            pltpu.VMEM((ATTR * BLOCK, 2 * CHUNK), BF),
            pltpu.VMEM((ATTR * BLOCK, 2 * CHUNK), BF),
            pltpu.VMEM((NBLK, 2 * CHUNK), BF),
            pltpu.VMEM((NBLK, 2 * CHUNK), BF),
            pltpu.VMEM((ATTR * BLOCK, NBLK), F32),
        ],
        2 * 2 * ATTR * BLOCK * NBLK * FLOC_DEV,
        floc_attr,
        slot_row,
        same_pairs.reshape(2, PSAME),
        same_count,
    )
    send = send.reshape(tiles, cap_blocks, ATTR, BLOCK)
    owned = lax.all_to_all(send, "tile", split_axis=0, concat_axis=0, tiled=True)
    owned = owned.reshape(NBLK, ATTR, BLOCK)
    up = lax.ppermute(owned[NBLK - EDGE :], "seg", [(i, i + 1) for i in range(segs - 1)])
    down = lax.ppermute(owned[:EDGE], "seg", [(i + 1, i) for i in range(segs - 1)])
    gain, adj_list = call(
        same_kernel,
        "same_pairs",
        (shape(NBLK, BLOCK), jax.ShapeDtypeStruct((2, PADJ), jnp.int32)),
        [VMEM, SMEM, VMEM],
        [
            pltpu.VMEM((GROUP, BLOCK, KF), BF),
            pltpu.VMEM((GROUP, BLOCK, KF), BF),
            pltpu.VMEM((GROUP + 2, KF, BLOCK), BF),
            pltpu.VMEM((GROUP + 2, KF, BLOCK), BF),
        ],
        40_000_000_000,
        owned,
        mult,
        adj_pairs.reshape(2, PADJ),
    )
    gain = call(
        adj_kernel,
        "adjacent_pairs",
        shape(NBLK, BLOCK),
        [VMEM, VMEM, VMEM, VMEM, SMEM, VMEM, SMEM],
        [
            pltpu.VMEM((2 * EDGE, BLOCK, KADJ), BF),
            pltpu.VMEM((2 * EDGE, KADJ, 2 * BLOCK), BF),
            pltpu.VMEM((PADJ, BLOCK), F32),
        ],
        10_000_000_000,
        owned,
        up,
        down,
        gain,
        adj_list,
        adj_list,
        neighbour_pair_count,
    )
    gain = gain.reshape(tiles, cap_blocks, BLOCK)
    returned = lax.all_to_all(gain, "tile", split_axis=0, concat_axis=0, tiled=True)
    out = call(
        gather_kernel,
        "final_gather",
        shape(1, FLOC_DEV),
        [VMEM, VMEM, VMEM],
        [],
        10_000_000_000,
        returned.reshape(NBLK, BLOCK),
        slot_row,
        floc_attr,
    )
    return out.reshape(FLOC_DEV)


def solution(mesh):
    placed = (
        P(None, ("seg", "tile")),
        P(("seg", "tile")),
        P("seg", "tile", None, None),
        P("seg", "tile"),
        P("seg", "tile", None, None),
        P("seg", "tile"),
    )
    return jax.shard_map(
        body, mesh=mesh, in_specs=placed, out_specs=P(("seg", "tile")), check_vma=False
    )
```
